32 devices in a mesh: inner: 16 (over z, y, core), outer: 2 (over x).
Axes of the slice: x: 2, y: 2, z: 4, core: 2. Of those that a mesh axis runs over, the one named last changes fastest.
Arguments:
- samples: float32 [2, 32, 262144], P(None, ('inner', 'outer')), may hold values from -6 to 6
- gram_index: int32 [1048576], P(('inner', 'outer')), may hold values from 0 to 7, as said below
- gram_offset: int32 [1048576], P(('inner', 'outer')), may hold values from 0 to 31
Outputs:
- z_field: float32 [8388608], P(('inner', 'outer'))
- gram_values: float32 [1048576], P(('inner', 'outer'))
The draws below stay inside these ranges and needn't reach their ends.
Inputs may be any that keep to these rules, and one draw needn't show every extreme that they name: `gram_index`: A device's first Gram point has 0 and its last 7.
All inputs are finite; a program needn't handle non-finite values.
Results may differ from the reference program's by a relative error of at most 0.00007.
Values sent between devices are 32-bit elements; how exact they have to be, the bound alone decides.
A program may use at most 256 MiB of HBM per device.

```python
import jax
import jax.numpy as jnp

SEG_DEV = 262144
GAP = 8
HALF = 16
UPS = 32
LENGTH = 8388608
GRAM_DEV = 32768
GRAMS = 1048576
DEVICES = 32


def draw_gram_index(key, part):
    device_rows = GRAMS // GRAM_DEV
    jitter = jax.random.randint(key, (device_rows, GRAM_DEV), 0, GAP)
    column = jnp.arange(GRAM_DEV, dtype=jnp.int32)[None, :]
    jitter = jnp.where(column == 0, 0, jitter)
    jitter = jnp.where(column == GRAM_DEV - 1, GAP - 1, jitter)
    return jitter.reshape(GRAMS).astype(jnp.int32)


def with_ends(result, key, smallest, largest):
    dims = result.shape
    spot = [jax.random.randint(jax.random.fold_in(key, axis), (), 0, dims[axis]) for axis in range(len(dims))]
    result = result.at[tuple(spot)].set(smallest)
    longest = dims.index(max(dims))
    spot[longest] = (spot[longest] + 1) % dims[longest]
    return result.at[tuple(spot)].set(largest)


def level_of(key, shape, shards, least, largest):
    def one(position, parts):
        draws = jax.random.uniform(jax.random.fold_in(jax.random.fold_in(key, 6), position), (parts,), jnp.float32, least / len(shards), largest / len(shards))
        return jnp.repeat(jnp.exp(draws), shape[position] // parts).reshape((-1,) + (1,) * (len(shape) - position - 1))

    gain = one(*shards[0])
    for cut in shards[1:]:
        gain = gain * one(*cut)
    return gain


def normal_values(rng, dims, deviation, limit, split=(), kind=jnp.bfloat16):
    level = level_of(rng, dims, split, -0.22, 0.18) if split else 1.0
    drawn = jax.random.normal(rng, dims, jnp.float32) * deviation * level
    return jnp.minimum(jnp.maximum(drawn, -limit), limit).astype(kind)


def setup_inputs(seed: int = 0) -> dict:
    key_list = jax.random.split(jax.random.key(seed), 4)
    return {
        "samples": normal_values(key_list[0], (2, DEVICES, SEG_DEV), 1.0, 6.0, ((1, 32),), jnp.float32),
        "gram_index": draw_gram_index(jax.random.fold_in(key_list[3], 71), 0),
        "gram_offset": with_ends(jax.random.randint(key_list[2], (GRAMS,), 0, UPS), jax.random.fold_in(key_list[2], 1), 0, UPS - 1).astype(jnp.int32),
    }


deconv_rate = 4.0


def window_weight(distance):
    spread = HALF / 2.0
    return jnp.sinc(distance) * jnp.exp(-distance * distance / (2.0 * spread * spread))


def reference(samples, gram_index, gram_offset):
    signal = jnp.transpose(samples, (0, 2, 1)).reshape(2, LENGTH)
    spectrum = jnp.fft.fft(signal[0] + 1j * signal[1])
    index_k = jnp.arange(LENGTH, dtype=jnp.int32)
    centred = (index_k // SEG_DEV).astype(jnp.float32) / DEVICES + (index_k % SEG_DEV).astype(jnp.float32) / LENGTH - 0.5
    z_field = jnp.real(spectrum).astype(jnp.float32) * (LENGTH ** -0.5) * jnp.exp(deconv_rate * centred * centred)
    padded = jnp.pad(z_field, HALF)
    point_ids = jnp.arange(GRAMS, dtype=jnp.int32)
    anchor = (point_ids // GRAM_DEV) * SEG_DEV + (point_ids % GRAM_DEV) * GAP + gram_index.astype(jnp.int32) + HALF
    fraction = gram_offset.astype(jnp.float32) / UPS
    gram_values = jnp.zeros((GRAMS,), jnp.float32)
    for offset in range(1 - HALF, HALF + 1):
        gram_values = gram_values + padded[anchor + offset] * window_weight(fraction - offset)
    return z_field, gram_values
```

```python
import functools
import math

import jax
import jax.numpy as jnp
import numpy as np
from jax import lax
from jax.experimental import pallas as pl
from jax.experimental.pallas import tpu as pltpu
from jax.sharding import PartitionSpec as P

GAP = 8
HALF = 16
UPS = 32
LANES = 128
RADIX = 8
STEPS = 256
TAU = 2.0 * math.pi
RATE = 4.0
MESH = pl.DeviceIdType.MESH
NT = (((1,), (1,)), ((), ()))


def halves(x):
    high = x.astype(jnp.bfloat16)
    low = (x - high.astype(jnp.float32)).astype(jnp.bfloat16)
    return high, low


def np_halves(x):
    x = x.astype(np.float32)
    high = x.astype(jnp.bfloat16)
    low = (x - high.astype(np.float32)).astype(jnp.bfloat16)
    return high, low


def stage_table():
    p = np.arange(RADIX)[:, None, None]
    f = np.arange(STEPS)[None, :, None]
    t = np.arange(STEPS)[None, None, :]
    order = RADIX * STEPS
    angle = (t * (RADIX * f + p) % order) * (-TAU / order)
    return np.stack([*np_halves(np.cos(angle)), *np_halves(np.sin(angle))], axis=1)


def order_table():
    size = GAP * LANES
    p, l = np.divmod(np.arange(size), LANES)
    table = np.zeros((size, size), np.float32)
    table[np.arange(size), GAP * l + p] = 1.0
    return table.astype(jnp.bfloat16)


def weight_table():
    tap = np.arange(1 - HALF, HALF + 1)[:, None]
    distance = np.arange(LANES)[None, :] % UPS / UPS - tap
    spread = HALF / 2.0
    table = np.sinc(distance) * np.exp(-distance * distance / (2.0 * spread * spread))
    return np.broadcast_to(table.astype(np.float32)[:, None, :], (2 * HALF, 8, LANES)).copy()


def radix_8(parts):
    def add(u, v):
        return u[0] + v[0], u[1] + v[1]

    def sub(u, v):
        return u[0] - v[0], u[1] - v[1]

    def turn(u):
        return u[1], -u[0]

    def four(a, b, c, d):
        s, t, u, v = add(a, c), sub(a, c), add(b, d), turn(sub(b, d))
        return add(s, u), add(t, v), sub(s, u), sub(t, v)

    even = four(parts[0], parts[2], parts[4], parts[6])
    odd = four(parts[1], parts[3], parts[5], parts[7])
    r = math.sqrt(0.5)
    odd = (
        odd[0],
        ((odd[1][0] + odd[1][1]) * r, (odd[1][1] - odd[1][0]) * r),
        turn(odd[2]),
        ((odd[3][1] - odd[3][0]) * r, -(odd[3][0] + odd[3][1]) * r),
    )
    return [add(e, o) for e, o in zip(even, odd)] + [sub(e, o) for e, o in zip(even, odd)]


def transform(values):
    size = len(values)
    if size == 1:
        return values
    even, odd = transform(values[0::2]), transform(values[1::2])
    first, second = [], []
    for k in range(size // 2):
        (er, ei), (br, bi) = even[k], odd[k]
        if k == 0:
            tr, ti = br, bi
        elif 4 * k == size:
            tr, ti = bi, -br
        else:
            c, s = math.cos(TAU * k / size), -math.sin(TAU * k / size)
            tr, ti = br * c - bi * s, br * s + bi * c
        first.append((er + tr, ei + ti))
        second.append((er - tr, ei - ti))
    return first + second


def real_transform(values):
    size = len(values)
    even, odd = transform(values[0::2]), transform(values[1::2])
    first, second = [], []
    for k in range(size // 2):
        c, s = math.cos(TAU * k / size), -math.sin(TAU * k / size)
        t = odd[k][0] if k == 0 else odd[k][1] if 4 * k == size else odd[k][0] * c - odd[k][1] * s
        first.append(even[k][0] + t)
        second.append(even[k][0] - t)
    return first + second


def across_kernel(
    inner, outer, x_ref, stage_ref, u_ref, v_ref, last_ref, out_ref, halo_ref,
    parts, rows, send_a, recv_a, send_b, edge, sem_sa, sem_ra, sem_sb, sem_rb, sem_se, sem_re,
):
    devices = inner * outer
    me = lax.axis_index("inner") * outer + lax.axis_index("outer")
    depth = send_a.shape[3]

    def where(device):
        return (device // outer, device % outer)

    def other(step):
        return (me + step) % devices

    barrier = pltpu.get_barrier_semaphore()

    @pl.loop(1, devices)
    def _(step):
        pl.semaphore_signal(barrier, inc=1, device_id=where(other(step)), device_id_type=MESH)

    @pl.loop(0, STEPS // 32)
    def _(tile):
        at = pl.ds(pl.multiple_of(tile * 32, 32), 32)
        done = radix_8([(x_ref[0, q, at], x_ref[1, q, at]) for q in range(RADIX)])
        for p in range(RADIX):
            parts[p, at, :LANES] = done[p][0]
            parts[p, at, LANES:] = done[p][1]

    def dot(a, b):
        return jnp.dot(a, b, preferred_element_type=jnp.float32)

    def dot_nt(a, b):
        return lax.dot_general(a, b, NT, preferred_element_type=jnp.float32)

    last_high, last_low = halves(last_ref[...])

    @pl.loop(0, RADIX)
    def _(p):
        high, low = halves(parts[p])
        cos_high, cos_low, sin_high, sin_low = (stage_ref[p, i] for i in range(4))
        by_cos = dot(cos_high, high) + dot(cos_high, low) + dot(cos_low, high)
        by_sin = dot(sin_high, high) + dot(sin_high, low) + dot(sin_low, high)
        real = by_cos[:, :LANES] - by_sin[:, LANES:]
        imag = by_cos[:, LANES:] + by_sin[:, :LANES]
        vr, vi = v_ref[0, pl.ds(p, 1)], v_ref[1, pl.ds(p, 1)]
        ur, ui = u_ref[0], u_ref[1]
        tr, ti = ur * vr - ui * vi, ur * vi + ui * vr
        both = jnp.concatenate([real * tr - imag * ti, real * ti + imag * tr], axis=1)
        high, low = halves(both)
        z = dot_nt(last_high, high) + dot_nt(last_high, low) + dot_nt(last_low, high)
        for part in range(2):
            block = z[part * LANES : (part + 1) * LANES]
            for side in range(2):
                rows[part, pl.ds(side, LANES, stride=2), :] = block[:, side * LANES : (side + 1) * LANES]
            send_a[:, part, p] = rows[part].reshape(devices, depth, LANES)

    pl.semaphore_wait(barrier, devices - 1)

    def copy_a(target, source):
        return pltpu.make_async_remote_copy(
            src_ref=send_a.at[target], dst_ref=recv_a.at[me],
            send_sem=sem_sa.at[target], recv_sem=sem_ra.at[source],
            device_id=where(target), device_id_type=MESH,
        )

    def copy_b(target, source):
        return pltpu.make_async_remote_copy(
            src_ref=send_b.at[target], dst_ref=out_ref.at[me],
            send_sem=sem_sb.at[target], recv_sem=sem_rb.at[source],
            device_id=where(target), device_id_type=MESH,
        )

    def copy_edge(target, side):
        shift = 1 if side else -1
        return pltpu.make_async_remote_copy(
            src_ref=edge.at[target + shift], dst_ref=halo_ref.at[side],
            send_sem=sem_se.at[target], recv_sem=sem_re.at[side],
            device_id=where(target), device_id_type=MESH,
        )

    @pl.loop(1, devices)
    def _(step):
        copy_a(other(step), me).start()

    recv_a[me] = send_a[me]

    @pl.loop(1, devices)
    def _(step):
        source = other(devices - step)
        copy_a(source, source).wait_recv()

    @pl.loop(0, RADIX)
    def _(p):
        values = [(recv_a[a, 0, p], recv_a[a, 1, p]) for a in range(devices)]
        done = real_transform(values)
        for k in range(devices):
            send_b[k, p] = done[k]

    def fill_edge(row):
        @pl.loop(0, devices)
        def _(k):
            edge[k] = send_b[k, :, row]

    @pl.when(me == 0)
    def _():
        fill_edge(0)

        @pl.loop(1, devices - 1)
        def _(target):
            copy_edge(target, 1).start()

    @pl.when(me == devices - 1)
    def _():
        fill_edge(depth - 1)

        @pl.loop(1, devices - 1)
        def _(target):
            copy_edge(target, 0).start()

    @pl.loop(1, devices)
    def _(step):
        copy_b(other(step), me).start()

    out_ref[me] = send_b[me]

    @pl.when(me == 0)
    def _():
        halo_ref[0] = jnp.zeros(halo_ref.shape[1:], jnp.float32)
        halo_ref[1] = edge[1]

    @pl.when(me == devices - 1)
    def _():
        halo_ref[0] = edge[devices - 2]
        halo_ref[1] = jnp.zeros(halo_ref.shape[1:], jnp.float32)

    @pl.loop(1, devices)
    def _(step):
        source = other(devices - step)
        copy_b(source, source).wait_recv()

    @pl.when(jnp.logical_and(me > 0, me < devices - 1))
    def _():
        copy_edge(me, 0).wait_recv()
        copy_edge(me, 1).wait_recv()

    @pl.when(jnp.logical_or(me == 0, me == devices - 1))
    def _():
        @pl.loop(1, devices - 1)
        def _(target):
            copy_edge(target, 0).wait_send()

    @pl.loop(1, devices)
    def _(step):
        copy_a(other(step), me).wait_send()
        copy_b(other(step), me).wait_send()


def across(samples, inner, outer):
    devices = inner * outer
    seg = samples.shape[2]
    length = seg * devices
    me = lax.axis_index("inner") * outer + lax.axis_index("outer")
    depth = seg // (devices * RADIX * LANES)
    x = samples.reshape(2, RADIX, STEPS, LANES)

    def phase(number, order):
        angle = number.astype(jnp.float32) * (-TAU / order)
        return jnp.cos(angle), jnp.sin(angle)

    f = lax.broadcasted_iota(jnp.int32, (STEPS, LANES), 0)
    u = jnp.stack(phase(f * (lax.broadcasted_iota(jnp.int32, (STEPS, LANES), 1) * devices + me), length // RADIX))
    p = lax.broadcasted_iota(jnp.int32, (RADIX, LANES), 0)
    v = jnp.stack(phase(p * (lax.broadcasted_iota(jnp.int32, (RADIX, LANES), 1) * devices + me), length))
    g = lax.broadcasted_iota(jnp.int32, (LANES, LANES), 0)
    order = LANES * devices
    number = g * (lax.broadcasted_iota(jnp.int32, (LANES, LANES), 1) * devices + me) % order
    cosine, sine = phase(number, order)
    last = jnp.concatenate(
        [jnp.concatenate([cosine, -sine], axis=1), jnp.concatenate([sine, cosine], axis=1)], axis=0
    )
    vmem = pl.BlockSpec(memory_space=pltpu.VMEM)
    block = (devices, RADIX, depth, LANES)
    return pl.pallas_call(
        functools.partial(across_kernel, inner, outer),
        out_shape=(
            jax.ShapeDtypeStruct(block, jnp.float32),
            jax.ShapeDtypeStruct((2, RADIX, LANES), jnp.float32),
        ),
        in_specs=[vmem] * 5,
        out_specs=(vmem, vmem),
        scratch_shapes=[
            pltpu.VMEM((RADIX, STEPS, 2 * LANES), jnp.float32),
            pltpu.VMEM((2, STEPS, LANES), jnp.float32),
            pltpu.VMEM((devices, 2, RADIX, depth, LANES), jnp.float32),
            pltpu.VMEM((devices, 2, RADIX, depth, LANES), jnp.float32),
            pltpu.VMEM(block, jnp.float32),
            pltpu.VMEM((devices, RADIX, LANES), jnp.float32),
        ]
        + [pltpu.SemaphoreType.DMA((devices,))] * 5
        + [pltpu.SemaphoreType.DMA((2,))],
        compiler_params=pltpu.CompilerParams(
            collective_id=0, has_side_effects=True, vmem_limit_bytes=48 * 2**20
        ),
    )(x, jnp.asarray(stage_table()), u, v, last)


def gram_kernel(inner, outer, real_ref, halo_ref, index_ref, offset_ref, weight_ref, order_ref, z_ref, gram_ref, field):
    devices = inner * outer
    depth = real_ref.shape[2]
    seg = STEPS * LANES * GAP
    length = seg * devices
    me = lax.axis_index("inner") * outer + lax.axis_index("outer")
    base = me.astype(jnp.float32) / devices - 0.5

    def scale(first_row, shape):
        row = lax.broadcasted_iota(jnp.int32, shape, 1) + first_row
        at = (row * LANES + lax.broadcasted_iota(jnp.int32, shape, 2)) * GAP + lax.broadcasted_iota(jnp.int32, shape, 0)
        centred = base + at.astype(jnp.float32) / length
        return jnp.exp(RATE * centred * centred) * length**-0.5

    @pl.loop(0, devices)
    def _(e):
        at = pl.ds(pl.multiple_of(8 + e * depth, depth), depth)
        field[:, at, :] = real_ref[e] * scale(e * depth, real_ref.shape[1:])

    field[:, 7:8, :] = halo_ref[0][:, None, :] * scale(-1, (GAP, 1, LANES))
    field[:, STEPS + 8 : STEPS + 9, :] = halo_ref[1][:, None, :] * scale(STEPS, (GAP, 1, LANES))

    lane = lax.broadcasted_iota(jnp.int32, (8, LANES), 1)

    @pl.loop(0, STEPS // 8)
    def _(tile):
        row = pl.multiple_of(tile * 8, 8)
        index = index_ref[pl.ds(row, 8)]
        offset = offset_ref[pl.ds(row, 8)]
        samples = {}
        for p in range(GAP):
            now = field[p, pl.ds(row + 8, 8)]
            before = field[p, pl.ds(row + 7, 8)]
            after = field[p, pl.ds(row + 9, 8)]
            for slot in (-2, -1, 0, 1, 2):
                place = GAP * slot + p
                if place < 1 - HALF or place > HALF + GAP - 1:
                    continue
                if slot < 0:
                    value = pltpu.roll(jnp.where(lane >= LANES + slot, before, now), -slot, 1)
                elif slot > 0:
                    value = pltpu.roll(jnp.where(lane < slot, after, now), LANES - slot, 1)
                else:
                    value = now
                samples[place] = value
        window = [samples[place] for place in range(1 - HALF, HALF + GAP)]
        for bit in (4, 2, 1):
            chosen = (index & bit) != 0
            window = [jnp.where(chosen, b, a) for a, b in zip(window[:-bit], window[bit:])]
        total = jnp.zeros((8, LANES), jnp.float32)
        for tap in range(2 * HALF):
            total += window[tap] * jnp.take_along_axis(weight_ref[tap], offset, axis=1)
        gram_ref[pl.ds(row, 8)] = total

    pieces = []
    rest = jnp.concatenate([field[p, 8 : STEPS + 8, :] for p in range(GAP)], axis=1)
    for _ in range(3):
        piece = rest.astype(jnp.bfloat16)
        pieces.append(piece)
        rest = rest - piece.astype(jnp.float32)
    width = 2 * LANES
    for column in range(GAP * LANES // width):
        table = order_ref[:, column * width : (column + 1) * width]
        block = sum(jnp.dot(piece, table, preferred_element_type=jnp.float32) for piece in reversed(pieces))
        for side in range(2):
            z_ref[pl.ds(2 * column + side, STEPS, stride=GAP), :] = block[:, side * LANES : (side + 1) * LANES]


def local(inner, outer, samples, gram_index, gram_offset):
    real, halo = across(samples, inner, outer)
    rows = (STEPS, LANES)
    z, gram = pl.pallas_call(
        functools.partial(gram_kernel, inner, outer),
        out_shape=(
            jax.ShapeDtypeStruct((STEPS * GAP, LANES), jnp.float32),
            jax.ShapeDtypeStruct(rows, jnp.float32),
        ),
        in_specs=[pl.BlockSpec(memory_space=pltpu.VMEM)] * 6,
        out_specs=(pl.BlockSpec(memory_space=pltpu.VMEM),) * 2,
        scratch_shapes=[pltpu.VMEM((GAP, STEPS + 16, LANES), jnp.float32)],
        compiler_params=pltpu.CompilerParams(vmem_limit_bytes=48 * 2**20),
    )(
        real, halo, gram_index.reshape(rows), gram_offset.reshape(rows),
        jnp.asarray(weight_table()), jnp.asarray(order_table()),
    )
    return z.reshape(-1), gram.reshape(-1)


def solution(mesh):
    return jax.shard_map(
        functools.partial(local, mesh.shape["inner"], mesh.shape["outer"]),
        mesh=mesh,
        in_specs=(P(None, ("inner", "outer"), None), P(("inner", "outer")), P(("inner", "outer"))),
        out_specs=(P(("inner", "outer")), P(("inner", "outer"))),
        check_vma=False,
    )
```

```python
import functools
import math

import jax
import jax.numpy as jnp
import numpy as np
from jax import lax
from jax.experimental import pallas as pl
from jax.experimental.pallas import tpu as pltpu
from jax.sharding import PartitionSpec as P

GAP = 8
HALF = 16
UPS = 32
LANES = 128
RADIX = 8
STEPS = 256
GROUPS = 4
TAU = 2.0 * math.pi
RATE = 4.0
MESH = pl.DeviceIdType.MESH
NT = (((1,), (1,)), ((), ()))


def halves(x):
    high = x.astype(jnp.bfloat16)
    low = (x - high.astype(jnp.float32)).astype(jnp.bfloat16)
    return high, low


def np_halves(x):
    x = x.astype(np.float32)
    high = x.astype(jnp.bfloat16)
    low = (x - high.astype(np.float32)).astype(jnp.bfloat16)
    return high, low


def stage_table():
    p = np.arange(RADIX)[:, None, None]
    f = np.arange(STEPS)[None, :, None]
    t = np.arange(STEPS)[None, None, :]
    order = RADIX * STEPS
    angle = (t * (RADIX * f + p) % order) * (-TAU / order)
    return np.stack([*np_halves(np.cos(angle)), *np_halves(np.sin(angle))], axis=1)


def order_table():
    size = GAP * LANES
    p, l = np.divmod(np.arange(size), LANES)
    table = np.zeros((size, size), np.float32)
    table[np.arange(size), GAP * l + p] = 1.0
    return table.astype(jnp.bfloat16)


def weight_table():
    tap = np.arange(1 - HALF, HALF + 1)[:, None]
    distance = np.arange(LANES)[None, :] % UPS / UPS - tap
    spread = HALF / 2.0
    table = np.sinc(distance) * np.exp(-distance * distance / (2.0 * spread * spread))
    return np.broadcast_to(table.astype(np.float32)[:, None, :], (2 * HALF, 8, LANES)).copy()


def radix_8(parts):
    def add(u, v):
        return u[0] + v[0], u[1] + v[1]

    def sub(u, v):
        return u[0] - v[0], u[1] - v[1]

    def turn(u):
        return u[1], -u[0]

    def four(a, b, c, d):
        s, t, u, v = add(a, c), sub(a, c), add(b, d), turn(sub(b, d))
        return add(s, u), add(t, v), sub(s, u), sub(t, v)

    even = four(parts[0], parts[2], parts[4], parts[6])
    odd = four(parts[1], parts[3], parts[5], parts[7])
    r = math.sqrt(0.5)
    odd = (
        odd[0],
        ((odd[1][0] + odd[1][1]) * r, (odd[1][1] - odd[1][0]) * r),
        turn(odd[2]),
        ((odd[3][1] - odd[3][0]) * r, -(odd[3][0] + odd[3][1]) * r),
    )
    return [add(e, o) for e, o in zip(even, odd)] + [sub(e, o) for e, o in zip(even, odd)]


def transform(values):
    size = len(values)
    if size == 1:
        return values
    even, odd = transform(values[0::2]), transform(values[1::2])
    first, second = [], []
    for k in range(size // 2):
        (er, ei), (br, bi) = even[k], odd[k]
        if k == 0:
            tr, ti = br, bi
        elif 4 * k == size:
            tr, ti = bi, -br
        else:
            c, s = math.cos(TAU * k / size), -math.sin(TAU * k / size)
            tr, ti = br * c - bi * s, br * s + bi * c
        first.append((er + tr, ei + ti))
        second.append((er - tr, ei - ti))
    return first + second


def real_transform(values):
    size = len(values)
    even, odd = transform(values[0::2]), transform(values[1::2])
    first, second = [], []
    for k in range(size // 2):
        c, s = math.cos(TAU * k / size), -math.sin(TAU * k / size)
        t = odd[k][0] if k == 0 else odd[k][1] if 4 * k == size else odd[k][0] * c - odd[k][1] * s
        first.append(even[k][0] + t)
        second.append(even[k][0] - t)
    return first + second


def across_kernel(
    inner, outer, x_ref, stage_ref, u_ref, v_ref, last_ref, out_ref, halo_ref,
    parts, rows, send_a, recv_a, send_b, edge, sem_sa, sem_ra, sem_sb, sem_rb, sem_se, sem_re,
):
    devices = inner * outer
    me = lax.axis_index("inner") * outer + lax.axis_index("outer")
    groups, half, _, per, depth, _ = send_a.shape
    side_of = me // half
    place = me % half

    def where(device):
        return (device // outer, device % outer)

    def near(step):
        return side_of * half + (place + step) % half

    def far(step):
        return (1 - side_of) * half + (place + step) % half

    barrier = pltpu.get_barrier_semaphore()

    @pl.loop(1, devices)
    def _(step):
        pl.semaphore_signal(barrier, inc=1, device_id=where((me + step) % devices), device_id_type=MESH)

    @pl.loop(0, STEPS // 32)
    def _(tile):
        at = pl.ds(pl.multiple_of(tile * 32, 32), 32)
        done = radix_8([(x_ref[0, q, at], x_ref[1, q, at]) for q in range(RADIX)])
        for p in range(RADIX):
            parts[p, at, :LANES] = done[p][0]
            parts[p, at, LANES:] = done[p][1]

    def dot(a, b):
        return jnp.dot(a, b, preferred_element_type=jnp.float32)

    def dot_nt(a, b):
        return lax.dot_general(a, b, NT, preferred_element_type=jnp.float32)

    def copy_a(group, target, source):
        return pltpu.make_async_remote_copy(
            src_ref=send_a.at[group, target % half], dst_ref=recv_a.at[group, place],
            send_sem=sem_sa.at[group, target % half], recv_sem=sem_ra.at[group, source % half],
            device_id=where(target), device_id_type=MESH,
        )

    def copy_b(group, target, source):
        return pltpu.make_async_remote_copy(
            src_ref=send_b.at[group, target], dst_ref=out_ref.at[group, me],
            send_sem=sem_sb.at[group, target], recv_sem=sem_rb.at[group, source],
            device_id=where(target), device_id_type=MESH,
        )

    def copy_edge(target, end, source_side):
        shift = 1 if end else -1
        return pltpu.make_async_remote_copy(
            src_ref=edge.at[target + shift], dst_ref=halo_ref.at[end, side_of],
            send_sem=sem_se.at[target], recv_sem=sem_re.at[end, source_side],
            device_id=where(target), device_id_type=MESH,
        )

    last_high, last_low = halves(last_ref[...])

    def spectrum(group, member):
        p = group * per + member
        high, low = halves(parts[p])
        cos_high, cos_low, sin_high, sin_low = (stage_ref[p, i] for i in range(4))
        by_cos = dot(cos_high, high) + dot(cos_high, low) + dot(cos_low, high)
        by_sin = dot(sin_high, high) + dot(sin_high, low) + dot(sin_low, high)
        real = by_cos[:, :LANES] - by_sin[:, LANES:]
        imag = by_cos[:, LANES:] + by_sin[:, :LANES]
        vr, vi = v_ref[0, pl.ds(p, 1)], v_ref[1, pl.ds(p, 1)]
        ur, ui = u_ref[0], u_ref[1]
        tr, ti = ur * vr - ui * vi, ur * vi + ui * vr
        both = jnp.concatenate([real * tr - imag * ti, real * ti + imag * tr], axis=1)
        high, low = halves(both)
        z = dot_nt(last_high, high) + dot_nt(last_high, low) + dot_nt(last_low, high)
        for part in range(2):
            block = z[part * LANES : (part + 1) * LANES]
            for lane_half in range(2):
                rows[part, pl.ds(lane_half, LANES, stride=2), :] = block[:, lane_half * LANES : (lane_half + 1) * LANES]
            send_a[group, :, part, member] = rows[part].reshape(half, depth, LANES)

    @pl.loop(0, groups)
    def _(group):
        @pl.loop(0, per)
        def _(member):
            spectrum(group, member)

        @pl.when(group == 0)
        def _():
            pl.semaphore_wait(barrier, devices - 1)

        @pl.loop(1, half)
        def _(step):
            copy_a(group, near(step), me).start()

        recv_a[group, place] = send_a[group, place]

    sign = (1 - 2 * side_of).astype(jnp.float32)

    def combine(group, member):
        values = [(recv_a[group, a, 0, member], recv_a[group, a, 1, member]) for a in range(half)]
        for k, done in enumerate(real_transform(values)):
            send_b[group, 2 * k, member] = done
        turned = []
        for a, (vr, vi) in enumerate(values):
            c, s = math.cos(TAU * a / devices), -math.sin(TAU * a / devices)
            cs, ss = sign * c, sign * s
            turned.append((vr * cs, vi * cs) if a == 0 else (vr * cs - vi * ss, vr * ss + vi * cs))
        for k, done in enumerate(real_transform(turned)):
            send_b[group, 2 * k + 1, member] = done

    def edges(end):
        row = 0 if end else depth - 1
        shift = 1 if end else -1

        @pl.loop(0, devices)
        def _(k):
            for group in range(groups):
                edge[k, group * per : (group + 1) * per] = send_b[group, k, :, row]

        @pl.loop(0, devices)
        def _(target):
            inside = jnp.logical_and(target + shift >= 0, target + shift < devices)

            @pl.when(jnp.logical_and(inside, target != me))
            def _():
                copy_edge(target, end, side_of).start()

    def edges_sent(end):
        shift = 1 if end else -1

        @pl.loop(0, devices)
        def _(target):
            inside = jnp.logical_and(target + shift >= 0, target + shift < devices)

            @pl.when(jnp.logical_and(inside, target != me))
            def _():
                copy_edge(target, end, side_of).wait_send()

    @pl.loop(0, groups)
    def _(group):
        @pl.loop(1, half)
        def _(step):
            source = near(half - step)
            copy_a(group, source, source).wait_recv()

        @pl.loop(0, per)
        def _(member):
            combine(group, member)

        @pl.when(group == groups - 1)
        def _():
            for end in range(2):
                @pl.when(place == (0 if end else half - 1))
                def _():
                    edges(end)

        @pl.loop(0, half)
        def _(step):
            copy_b(group, far(step), me).start()

        @pl.loop(1, half)
        def _(step):
            copy_b(group, near(step), me).start()

        out_ref[group, me] = send_b[group, me]

    for end in range(2):
        sender = 0 if end else half - 1
        bound = devices - 1 if end else 0
        shift = 1 if end else -1

        @pl.when(me == bound)
        def _():
            halo_ref[end] = jnp.zeros(halo_ref.shape[1:], jnp.float32)

        @pl.when(me != bound)
        def _():
            for source_side in range(2):
                source = source_side * half + sender

                @pl.when(me == source)
                def _():
                    halo_ref[end, source_side] = edge[me + shift]

                @pl.when(me != source)
                def _():
                    copy_edge(me, end, source_side).wait_recv()

    @pl.loop(0, groups)
    def _(group):
        @pl.loop(1, devices)
        def _(step):
            source = (me + devices - step) % devices
            copy_b(group, source, source).wait_recv()

    for end in range(2):
        @pl.when(place == (0 if end else half - 1))
        def _():
            edges_sent(end)

    @pl.loop(0, groups)
    def _(group):
        @pl.loop(1, half)
        def _(step):
            copy_a(group, near(step), me).wait_send()

        @pl.loop(1, devices)
        def _(step):
            copy_b(group, (me + step) % devices, me).wait_send()


def across(samples, inner, outer):
    devices = inner * outer
    seg = samples.shape[2]
    length = seg * devices
    me = lax.axis_index("inner") * outer + lax.axis_index("outer")
    half = devices // 2
    depth = STEPS // half
    per = RADIX // GROUPS
    x = samples.reshape(2, RADIX, STEPS, LANES)

    def phase(number, order):
        angle = number.astype(jnp.float32) * (-TAU / order)
        return jnp.cos(angle), jnp.sin(angle)

    f = lax.broadcasted_iota(jnp.int32, (STEPS, LANES), 0)
    u = jnp.stack(phase(f * (lax.broadcasted_iota(jnp.int32, (STEPS, LANES), 1) * devices + me), length // RADIX))
    p = lax.broadcasted_iota(jnp.int32, (RADIX, LANES), 0)
    v = jnp.stack(phase(p * (lax.broadcasted_iota(jnp.int32, (RADIX, LANES), 1) * devices + me), length))
    g = lax.broadcasted_iota(jnp.int32, (LANES, LANES), 0)
    order = LANES * devices
    number = g * (lax.broadcasted_iota(jnp.int32, (LANES, LANES), 1) * devices + me) % order
    cosine, sine = phase(number, order)
    last = jnp.concatenate(
        [jnp.concatenate([cosine, -sine], axis=1), jnp.concatenate([sine, cosine], axis=1)], axis=0
    )
    vmem = pl.BlockSpec(memory_space=pltpu.VMEM)
    first = (GROUPS, half, 2, per, depth, LANES)
    block = (GROUPS, devices, per, depth, LANES)
    return pl.pallas_call(
        functools.partial(across_kernel, inner, outer),
        out_shape=(
            jax.ShapeDtypeStruct(block, jnp.float32),
            jax.ShapeDtypeStruct((2, 2, RADIX, LANES), jnp.float32),
        ),
        in_specs=[vmem] * 5,
        out_specs=(vmem, vmem),
        scratch_shapes=[
            pltpu.VMEM((RADIX, STEPS, 2 * LANES), jnp.float32),
            pltpu.VMEM((2, STEPS, LANES), jnp.float32),
            pltpu.VMEM(first, jnp.float32),
            pltpu.VMEM(first, jnp.float32),
            pltpu.VMEM(block, jnp.float32),
            pltpu.VMEM((devices, RADIX, LANES), jnp.float32),
        ]
        + [pltpu.SemaphoreType.DMA((GROUPS, half))] * 2
        + [pltpu.SemaphoreType.DMA((GROUPS, devices))] * 2
        + [pltpu.SemaphoreType.DMA((devices,)), pltpu.SemaphoreType.DMA((2, 2))],
        compiler_params=pltpu.CompilerParams(
            collective_id=0, has_side_effects=True, vmem_limit_bytes=48 * 2**20
        ),
    )(x, jnp.asarray(stage_table()), u, v, last)


def gram_kernel(inner, outer, real_ref, halo_ref, index_ref, offset_ref, weight_ref, order_ref, z_ref, gram_ref, field):
    devices = inner * outer
    groups, _, per, depth, _ = real_ref.shape
    half = devices // 2
    seg = STEPS * LANES * GAP
    length = seg * devices
    me = lax.axis_index("inner") * outer + lax.axis_index("outer")
    base = me.astype(jnp.float32) / devices - 0.5

    def scale(first_row, shape):
        row = lax.broadcasted_iota(jnp.int32, shape, 1) + first_row
        at = (row * LANES + lax.broadcasted_iota(jnp.int32, shape, 2)) * GAP + lax.broadcasted_iota(jnp.int32, shape, 0)
        centred = base + at.astype(jnp.float32) / length
        return jnp.exp(RATE * centred * centred) * length**-0.5

    @pl.loop(0, half)
    def _(e):
        at = pl.ds(pl.multiple_of(8 + e * depth, math.gcd(8, depth)), depth)
        factor = scale(e * depth, (GAP, depth, LANES))
        for group in range(groups):
            members = slice(group * per, (group + 1) * per)
            field[members, at, :] = (real_ref[group, e] + real_ref[group, half + e]) * factor[members]

    halo = halo_ref[:, 0] + halo_ref[:, 1]
    field[:, 7:8, :] = halo[0][:, None, :] * scale(-1, (GAP, 1, LANES))
    field[:, STEPS + 8 : STEPS + 9, :] = halo[1][:, None, :] * scale(STEPS, (GAP, 1, LANES))

    lane = lax.broadcasted_iota(jnp.int32, (8, LANES), 1)

    @pl.loop(0, STEPS // 8)
    def _(tile):
        row = pl.multiple_of(tile * 8, 8)
        index = index_ref[pl.ds(row, 8)]
        offset = offset_ref[pl.ds(row, 8)]
        samples = {}
        for p in range(GAP):
            now = field[p, pl.ds(row + 8, 8)]
            before = field[p, pl.ds(row + 7, 8)]
            after = field[p, pl.ds(row + 9, 8)]
            for slot in (-2, -1, 0, 1, 2):
                place = GAP * slot + p
                if place < 1 - HALF or place > HALF + GAP - 1:
                    continue
                if slot < 0:
                    value = pltpu.roll(jnp.where(lane >= LANES + slot, before, now), -slot, 1)
                elif slot > 0:
                    value = pltpu.roll(jnp.where(lane < slot, after, now), LANES - slot, 1)
                else:
                    value = now
                samples[place] = value
        window = [samples[place] for place in range(1 - HALF, HALF + GAP)]
        for bit in (4, 2, 1):
            chosen = (index & bit) != 0
            window = [jnp.where(chosen, b, a) for a, b in zip(window[:-bit], window[bit:])]
        total = jnp.zeros((8, LANES), jnp.float32)
        for tap in range(2 * HALF):
            total += window[tap] * jnp.take_along_axis(weight_ref[tap], offset, axis=1)
        gram_ref[pl.ds(row, 8)] = total

    pieces = []
    rest = jnp.concatenate([field[p, 8 : STEPS + 8, :] for p in range(GAP)], axis=1)
    for _ in range(3):
        piece = rest.astype(jnp.bfloat16)
        pieces.append(piece)
        rest = rest - piece.astype(jnp.float32)
    width = 2 * LANES
    for column in range(GAP * LANES // width):
        table = order_ref[:, column * width : (column + 1) * width]
        block = sum(jnp.dot(piece, table, preferred_element_type=jnp.float32) for piece in reversed(pieces))
        for side in range(2):
            z_ref[pl.ds(2 * column + side, STEPS, stride=GAP), :] = block[:, side * LANES : (side + 1) * LANES]


def local(inner, outer, samples, gram_index, gram_offset):
    real, halo = across(samples, inner, outer)
    rows = (STEPS, LANES)
    z, gram = pl.pallas_call(
        functools.partial(gram_kernel, inner, outer),
        out_shape=(
            jax.ShapeDtypeStruct((STEPS * GAP, LANES), jnp.float32),
            jax.ShapeDtypeStruct(rows, jnp.float32),
        ),
        in_specs=[pl.BlockSpec(memory_space=pltpu.VMEM)] * 6,
        out_specs=(pl.BlockSpec(memory_space=pltpu.VMEM),) * 2,
        scratch_shapes=[pltpu.VMEM((GAP, STEPS + 16, LANES), jnp.float32)],
        compiler_params=pltpu.CompilerParams(vmem_limit_bytes=48 * 2**20),
    )(
        real, halo, gram_index.reshape(rows), gram_offset.reshape(rows),
        jnp.asarray(weight_table()), jnp.asarray(order_table()),
    )
    return z.reshape(-1), gram.reshape(-1)


def solution(mesh):
    return jax.shard_map(
        functools.partial(local, mesh.shape["inner"], mesh.shape["outer"]),
        mesh=mesh,
        in_specs=(P(None, ("inner", "outer"), None), P(("inner", "outer")), P(("inner", "outer"))),
        out_specs=(P(("inner", "outer")), P(("inner", "outer"))),
        check_vma=False,
    )
```

```python
import functools
import math

import jax
import jax.numpy as jnp
import numpy as np
from jax import lax
from jax.experimental import pallas as pl
from jax.experimental.pallas import tpu as pltpu
from jax.sharding import PartitionSpec as P

GAP = 8
HALF = 16
UPS = 32
LANES = 128
RADIX = 8
STEPS = 256
GROUPS = 8
AHEAD = 2
TAU = 2.0 * math.pi
RATE = 4.0
MESH = pl.DeviceIdType.MESH
NT = (((1,), (1,)), ((), ()))


def halves(x):
    high = x.astype(jnp.bfloat16)
    low = (x - high.astype(jnp.float32)).astype(jnp.bfloat16)
    return high, low


def np_halves(x):
    x = x.astype(np.float32)
    high = x.astype(jnp.bfloat16)
    low = (x - high.astype(np.float32)).astype(jnp.bfloat16)
    return high, low


def stage_table():
    p = np.arange(RADIX)[:, None, None]
    f = np.arange(STEPS)[None, :, None]
    t = np.arange(STEPS)[None, None, :]
    order = RADIX * STEPS
    angle = (t * (RADIX * f + p) % order) * (-TAU / order)
    return np.stack([*np_halves(np.cos(angle)), *np_halves(np.sin(angle))], axis=1)


def order_table():
    size = GAP * LANES
    p, l = np.divmod(np.arange(size), LANES)
    table = np.zeros((size, size), np.float32)
    table[np.arange(size), GAP * l + p] = 1.0
    return table.astype(jnp.bfloat16)


def weight_table():
    tap = np.arange(1 - HALF, HALF + 1)[:, None]
    distance = np.arange(LANES)[None, :] % UPS / UPS - tap
    spread = HALF / 2.0
    table = np.sinc(distance) * np.exp(-distance * distance / (2.0 * spread * spread))
    return np.broadcast_to(table.astype(np.float32)[:, None, :], (2 * HALF, 8, LANES)).copy()


def radix_8(parts):
    def add(u, v):
        return u[0] + v[0], u[1] + v[1]

    def sub(u, v):
        return u[0] - v[0], u[1] - v[1]

    def turn(u):
        return u[1], -u[0]

    def four(a, b, c, d):
        s, t, u, v = add(a, c), sub(a, c), add(b, d), turn(sub(b, d))
        return add(s, u), add(t, v), sub(s, u), sub(t, v)

    even = four(parts[0], parts[2], parts[4], parts[6])
    odd = four(parts[1], parts[3], parts[5], parts[7])
    r = math.sqrt(0.5)
    odd = (
        odd[0],
        ((odd[1][0] + odd[1][1]) * r, (odd[1][1] - odd[1][0]) * r),
        turn(odd[2]),
        ((odd[3][1] - odd[3][0]) * r, -(odd[3][0] + odd[3][1]) * r),
    )
    return [add(e, o) for e, o in zip(even, odd)] + [sub(e, o) for e, o in zip(even, odd)]


def transform(values):
    size = len(values)
    if size == 1:
        return values
    even, odd = transform(values[0::2]), transform(values[1::2])
    first, second = [], []
    for k in range(size // 2):
        (er, ei), (br, bi) = even[k], odd[k]
        if k == 0:
            tr, ti = br, bi
        elif 4 * k == size:
            tr, ti = bi, -br
        else:
            c, s = math.cos(TAU * k / size), -math.sin(TAU * k / size)
            tr, ti = br * c - bi * s, br * s + bi * c
        first.append((er + tr, ei + ti))
        second.append((er - tr, ei - ti))
    return first + second


def real_transform(values):
    size = len(values)
    even, odd = transform(values[0::2]), transform(values[1::2])
    first, second = [], []
    for k in range(size // 2):
        c, s = math.cos(TAU * k / size), -math.sin(TAU * k / size)
        t = odd[k][0] if k == 0 else odd[k][1] if 4 * k == size else odd[k][0] * c - odd[k][1] * s
        first.append(even[k][0] + t)
        second.append(even[k][0] - t)
    return first + second


def across_kernel(
    inner, outer, x_ref, stage_ref, u_ref, v_ref, last_ref, out_ref, halo_ref,
    parts, rows, send_a, recv_a, send_b, edge, sem_sa, sem_ra, sem_sb, sem_rb, sem_se, sem_re,
):
    devices = inner * outer
    me = lax.axis_index("inner") * outer + lax.axis_index("outer")
    groups, half, _, per, depth, _ = send_a.shape
    side_of = me // half
    place = me % half

    def where(device):
        return (device // outer, device % outer)

    def near(step):
        return side_of * half + (place + step) % half

    def far(step):
        return (1 - side_of) * half + (place + step) % half

    barrier = pltpu.get_barrier_semaphore()

    @pl.loop(1, devices)
    def _(step):
        pl.semaphore_signal(barrier, inc=1, device_id=where((me + step) % devices), device_id_type=MESH)

    @pl.loop(0, STEPS // 32)
    def _(tile):
        at = pl.ds(pl.multiple_of(tile * 32, 32), 32)
        done = radix_8([(x_ref[0, q, at], x_ref[1, q, at]) for q in range(RADIX)])
        for p in range(RADIX):
            parts[p, at, :LANES] = done[p][0]
            parts[p, at, LANES:] = done[p][1]

    def dot(a, b):
        return jnp.dot(a, b, preferred_element_type=jnp.float32)

    def dot_nt(a, b):
        return lax.dot_general(a, b, NT, preferred_element_type=jnp.float32)

    def copy_a(group, target):
        return pltpu.make_async_remote_copy(
            src_ref=send_a.at[group, target % half], dst_ref=recv_a.at[group, place],
            send_sem=sem_sa.at[group], recv_sem=sem_ra.at[group],
            device_id=where(target), device_id_type=MESH,
        )

    def copy_b(group, target):
        return pltpu.make_async_remote_copy(
            src_ref=send_b.at[group, target], dst_ref=out_ref.at[group, me],
            send_sem=sem_sb.at[group], recv_sem=sem_rb.at[group],
            device_id=where(target), device_id_type=MESH,
        )

    def whole(ref, group, sem_sent, sem_here):
        count = ref.shape[1] - 1
        return pltpu.make_async_remote_copy(
            src_ref=ref.at[group, pl.ds(0, count)], dst_ref=ref.at[group, pl.ds(0, count)],
            send_sem=sem_sent.at[group], recv_sem=sem_here.at[group],
            device_id=where((me + 1) % devices), device_id_type=MESH,
        )

    def copy_edge(target, end, source_side):
        shift = 1 if end else -1
        return pltpu.make_async_remote_copy(
            src_ref=edge.at[target + shift], dst_ref=halo_ref.at[end, side_of],
            send_sem=sem_se.at[target], recv_sem=sem_re.at[end, source_side],
            device_id=where(target), device_id_type=MESH,
        )

    last_high, last_low = halves(last_ref[...])

    def spectrum(group, member):
        p = group * per + member
        high, low = halves(parts[p])
        cos_high, cos_low, sin_high, sin_low = (stage_ref[p, i] for i in range(4))
        by_cos = dot(cos_high, high) + dot(cos_high, low) + dot(cos_low, high)
        by_sin = dot(sin_high, high) + dot(sin_high, low) + dot(sin_low, high)
        real = by_cos[:, :LANES] - by_sin[:, LANES:]
        imag = by_cos[:, LANES:] + by_sin[:, :LANES]
        vr, vi = v_ref[0, pl.ds(p, 1)], v_ref[1, pl.ds(p, 1)]
        ur, ui = u_ref[0], u_ref[1]
        tr, ti = ur * vr - ui * vi, ur * vi + ui * vr
        both = jnp.concatenate([real * tr - imag * ti, real * ti + imag * tr], axis=1)
        high, low = halves(both)
        z = dot_nt(last_high, high) + dot_nt(last_high, low) + dot_nt(last_low, high)
        for part in range(2):
            block = z[part * LANES : (part + 1) * LANES]
            for lane_half in range(2):
                rows[part, pl.ds(lane_half, LANES, stride=2), :] = block[:, lane_half * LANES : (lane_half + 1) * LANES]
            send_a[group, :, part, member] = rows[part].reshape(half, depth, LANES)

    def spectra(group):
        @pl.loop(0, per)
        def _(member):
            spectrum(group, member)

        recv_a[group, place] = send_a[group, place]

    spectra(0)
    pl.semaphore_wait(barrier, devices - 1)

    @pl.loop(0, AHEAD)
    def _(group):
        @pl.when(group > 0)
        def _():
            spectra(group)

        @pl.loop(1, half)
        def _(step):
            copy_a(group, near(step)).start()

    sign = (1 - 2 * side_of).astype(jnp.float32)

    def combine(group, member):
        values = [(recv_a[group, a, 0, member], recv_a[group, a, 1, member]) for a in range(half)]
        for k, done in enumerate(real_transform(values)):
            send_b[group, 2 * k, member] = done
        turned = []
        for a, (vr, vi) in enumerate(values):
            c, s = math.cos(TAU * a / devices), -math.sin(TAU * a / devices)
            cs, ss = sign * c, sign * s
            turned.append((vr * cs, vi * cs) if a == 0 else (vr * cs - vi * ss, vr * ss + vi * cs))
        for k, done in enumerate(real_transform(turned)):
            send_b[group, 2 * k + 1, member] = done

    def edges(end):
        row = 0 if end else depth - 1
        shift = 1 if end else -1

        @pl.loop(0, devices)
        def _(k):
            for group in range(groups):
                edge[k, group * per : (group + 1) * per] = send_b[group, k, :, row]

        @pl.loop(0, devices)
        def _(target):
            inside = jnp.logical_and(target + shift >= 0, target + shift < devices)

            @pl.when(jnp.logical_and(inside, target != me))
            def _():
                copy_edge(target, end, side_of).start()

    def edges_sent(end):
        shift = 1 if end else -1

        @pl.loop(0, devices)
        def _(target):
            inside = jnp.logical_and(target + shift >= 0, target + shift < devices)

            @pl.when(jnp.logical_and(inside, target != me))
            def _():
                copy_edge(target, end, side_of).wait_send()

    @pl.loop(0, groups)
    def _(group):
        @pl.when(group + AHEAD < groups)
        def _():
            spectra(group + AHEAD)

        whole(recv_a, group, sem_sa, sem_ra).wait_recv()

        @pl.loop(0, per)
        def _(member):
            combine(group, member)

        @pl.when(group == groups - 1)
        def _():
            for end in range(2):
                @pl.when(place == (0 if end else half - 1))
                def _():
                    edges(end)

        copy_b(group, far(0)).start()

        @pl.loop(1, half)
        def _(step):
            copy_b(group, far(step)).start()
            copy_b(group, near(step)).start()

            @pl.when(group + AHEAD < groups)
            def _():
                copy_a(group + AHEAD, near(step)).start()

        out_ref[group, me] = send_b[group, me]

    for end in range(2):
        sender = 0 if end else half - 1
        bound = devices - 1 if end else 0
        shift = 1 if end else -1

        @pl.when(me == bound)
        def _():
            halo_ref[end] = jnp.zeros(halo_ref.shape[1:], jnp.float32)

        @pl.when(me != bound)
        def _():
            for source_side in range(2):
                source = source_side * half + sender

                @pl.when(me == source)
                def _():
                    halo_ref[end, source_side] = edge[me + shift]

                @pl.when(me != source)
                def _():
                    copy_edge(me, end, source_side).wait_recv()

    @pl.loop(0, groups)
    def _(group):
        whole(out_ref, group, sem_sb, sem_rb).wait_recv()

    for end in range(2):
        @pl.when(place == (0 if end else half - 1))
        def _():
            edges_sent(end)

    @pl.loop(0, groups)
    def _(group):
        whole(send_a, group, sem_sa, sem_ra).wait_send()
        whole(send_b, group, sem_sb, sem_rb).wait_send()


def across(samples, inner, outer):
    devices = inner * outer
    seg = samples.shape[2]
    length = seg * devices
    me = lax.axis_index("inner") * outer + lax.axis_index("outer")
    half = devices // 2
    depth = STEPS // half
    per = RADIX // GROUPS
    x = samples.reshape(2, RADIX, STEPS, LANES)

    def phase(number, order):
        angle = number.astype(jnp.float32) * (-TAU / order)
        return jnp.cos(angle), jnp.sin(angle)

    f = lax.broadcasted_iota(jnp.int32, (STEPS, LANES), 0)
    u = jnp.stack(phase(f * (lax.broadcasted_iota(jnp.int32, (STEPS, LANES), 1) * devices + me), length // RADIX))
    p = lax.broadcasted_iota(jnp.int32, (RADIX, LANES), 0)
    v = jnp.stack(phase(p * (lax.broadcasted_iota(jnp.int32, (RADIX, LANES), 1) * devices + me), length))
    g = lax.broadcasted_iota(jnp.int32, (LANES, LANES), 0)
    order = LANES * devices
    number = g * (lax.broadcasted_iota(jnp.int32, (LANES, LANES), 1) * devices + me) % order
    cosine, sine = phase(number, order)
    last = jnp.concatenate(
        [jnp.concatenate([cosine, -sine], axis=1), jnp.concatenate([sine, cosine], axis=1)], axis=0
    )
    vmem = pl.BlockSpec(memory_space=pltpu.VMEM)
    first = (GROUPS, half, 2, per, depth, LANES)
    block = (GROUPS, devices, per, depth, LANES)
    return pl.pallas_call(
        functools.partial(across_kernel, inner, outer),
        out_shape=(
            jax.ShapeDtypeStruct(block, jnp.float32),
            jax.ShapeDtypeStruct((2, 2, RADIX, LANES), jnp.float32),
        ),
        in_specs=[vmem] * 5,
        out_specs=(vmem, vmem),
        scratch_shapes=[
            pltpu.VMEM((RADIX, STEPS, 2 * LANES), jnp.float32),
            pltpu.VMEM((2, STEPS, LANES), jnp.float32),
            pltpu.VMEM(first, jnp.float32),
            pltpu.VMEM(first, jnp.float32),
            pltpu.VMEM(block, jnp.float32),
            pltpu.VMEM((devices, RADIX, LANES), jnp.float32),
        ]
        + [pltpu.SemaphoreType.DMA((GROUPS,))] * 4
        + [pltpu.SemaphoreType.DMA((devices,)), pltpu.SemaphoreType.DMA((2, 2))],
        compiler_params=pltpu.CompilerParams(
            collective_id=0, has_side_effects=True, vmem_limit_bytes=48 * 2**20
        ),
    )(x, jnp.asarray(stage_table()), u, v, last)


def gram_kernel(inner, outer, real_ref, halo_ref, index_ref, offset_ref, weight_ref, order_ref, z_ref, gram_ref, field):
    devices = inner * outer
    groups, _, per, depth, _ = real_ref.shape
    half = devices // 2
    seg = STEPS * LANES * GAP
    length = seg * devices
    me = lax.axis_index("inner") * outer + lax.axis_index("outer")
    base = me.astype(jnp.float32) / devices - 0.5

    def scale(first_row, shape):
        row = lax.broadcasted_iota(jnp.int32, shape, 1) + first_row
        at = (row * LANES + lax.broadcasted_iota(jnp.int32, shape, 2)) * GAP + lax.broadcasted_iota(jnp.int32, shape, 0)
        centred = base + at.astype(jnp.float32) / length
        return jnp.exp(RATE * centred * centred) * length**-0.5

    @pl.loop(0, half)
    def _(e):
        at = pl.ds(pl.multiple_of(8 + e * depth, math.gcd(8, depth)), depth)
        factor = scale(e * depth, (GAP, depth, LANES))
        for group in range(groups):
            members = slice(group * per, (group + 1) * per)
            field[members, at, :] = (real_ref[group, e] + real_ref[group, half + e]) * factor[members]

    halo = halo_ref[:, 0] + halo_ref[:, 1]
    field[:, 7:8, :] = halo[0][:, None, :] * scale(-1, (GAP, 1, LANES))
    field[:, STEPS + 8 : STEPS + 9, :] = halo[1][:, None, :] * scale(STEPS, (GAP, 1, LANES))

    lane = lax.broadcasted_iota(jnp.int32, (8, LANES), 1)

    @pl.loop(0, STEPS // 8)
    def _(tile):
        row = pl.multiple_of(tile * 8, 8)
        index = index_ref[pl.ds(row, 8)]
        offset = offset_ref[pl.ds(row, 8)]
        samples = {}
        for p in range(GAP):
            now = field[p, pl.ds(row + 8, 8)]
            before = field[p, pl.ds(row + 7, 8)]
            after = field[p, pl.ds(row + 9, 8)]
            for slot in (-2, -1, 0, 1, 2):
                place = GAP * slot + p
                if place < 1 - HALF or place > HALF + GAP - 1:
                    continue
                if slot < 0:
                    value = pltpu.roll(jnp.where(lane >= LANES + slot, before, now), -slot, 1)
                elif slot > 0:
                    value = pltpu.roll(jnp.where(lane < slot, after, now), LANES - slot, 1)
                else:
                    value = now
                samples[place] = value
        window = [samples[place] for place in range(1 - HALF, HALF + GAP)]
        for bit in (4, 2, 1):
            chosen = (index & bit) != 0
            window = [jnp.where(chosen, b, a) for a, b in zip(window[:-bit], window[bit:])]
        total = jnp.zeros((8, LANES), jnp.float32)
        for tap in range(2 * HALF):
            total += window[tap] * jnp.take_along_axis(weight_ref[tap], offset, axis=1)
        gram_ref[pl.ds(row, 8)] = total

    pieces = []
    rest = jnp.concatenate([field[p, 8 : STEPS + 8, :] for p in range(GAP)], axis=1)
    for _ in range(3):
        piece = rest.astype(jnp.bfloat16)
        pieces.append(piece)
        rest = rest - piece.astype(jnp.float32)
    width = 2 * LANES
    for column in range(GAP * LANES // width):
        table = order_ref[:, column * width : (column + 1) * width]
        block = sum(jnp.dot(piece, table, preferred_element_type=jnp.float32) for piece in reversed(pieces))
        for side in range(2):
            z_ref[pl.ds(2 * column + side, STEPS, stride=GAP), :] = block[:, side * LANES : (side + 1) * LANES]


def local(inner, outer, samples, gram_index, gram_offset):
    real, halo = across(samples, inner, outer)
    rows = (STEPS, LANES)
    z, gram = pl.pallas_call(
        functools.partial(gram_kernel, inner, outer),
        out_shape=(
            jax.ShapeDtypeStruct((STEPS * GAP, LANES), jnp.float32),
            jax.ShapeDtypeStruct(rows, jnp.float32),
        ),
        in_specs=[pl.BlockSpec(memory_space=pltpu.VMEM)] * 6,
        out_specs=(pl.BlockSpec(memory_space=pltpu.VMEM),) * 2,
        scratch_shapes=[pltpu.VMEM((GAP, STEPS + 16, LANES), jnp.float32)],
        compiler_params=pltpu.CompilerParams(vmem_limit_bytes=48 * 2**20),
    )(
        real, halo, gram_index.reshape(rows), gram_offset.reshape(rows),
        jnp.asarray(weight_table()), jnp.asarray(order_table()),
    )
    return z.reshape(-1), gram.reshape(-1)


def solution(mesh):
    return jax.shard_map(
        functools.partial(local, mesh.shape["inner"], mesh.shape["outer"]),
        mesh=mesh,
        in_specs=(P(None, ("inner", "outer"), None), P(("inner", "outer")), P(("inner", "outer"))),
        out_specs=(P(("inner", "outer")), P(("inner", "outer"))),
        check_vma=False,
    )
```

```python
import functools
import math

import jax
import jax.numpy as jnp
import numpy as np
from jax import lax
from jax.experimental import pallas as pl
from jax.experimental.pallas import tpu as pltpu
from jax.sharding import PartitionSpec as P

GAP = 8
HALF = 16
UPS = 32
LANES = 128
RADIX = 8
STEPS = 256
GROUPS = 8
AHEAD = 2
TAU = 2.0 * math.pi
RATE = 4.0
MESH = pl.DeviceIdType.MESH
NT = (((1,), (1,)), ((), ()))


def halves(x):
    high = x.astype(jnp.bfloat16)
    low = (x - high.astype(jnp.float32)).astype(jnp.bfloat16)
    return high, low


def np_halves(x):
    x = x.astype(np.float32)
    high = x.astype(jnp.bfloat16)
    low = (x - high.astype(np.float32)).astype(jnp.bfloat16)
    return high, low


def stage_table():
    p = np.arange(RADIX)[:, None, None]
    f = np.arange(STEPS)[None, :, None]
    t = np.arange(STEPS)[None, None, :]
    order = RADIX * STEPS
    angle = (t * (RADIX * f + p) % order) * (-TAU / order)
    return np.stack([*np_halves(np.cos(angle)), *np_halves(np.sin(angle))], axis=1)


def order_table():
    size = 2 * LANES
    p, l = np.divmod(np.arange(size), size // GAP)
    table = np.zeros((size, size), np.float32)
    table[np.arange(size), GAP * l + p] = 1.0
    return table.astype(jnp.bfloat16)


def weight_table():
    tap = np.arange(1 - HALF, HALF + 1)[:, None]
    distance = np.arange(LANES)[None, :] % UPS / UPS - tap
    spread = HALF / 2.0
    table = np.sinc(distance) * np.exp(-distance * distance / (2.0 * spread * spread))
    return np.broadcast_to(table.astype(np.float32)[:, None, :], (2 * HALF, 8, LANES)).copy()


def radix_8(parts):
    def add(u, v):
        return u[0] + v[0], u[1] + v[1]

    def sub(u, v):
        return u[0] - v[0], u[1] - v[1]

    def turn(u):
        return u[1], -u[0]

    def four(a, b, c, d):
        s, t, u, v = add(a, c), sub(a, c), add(b, d), turn(sub(b, d))
        return add(s, u), add(t, v), sub(s, u), sub(t, v)

    even = four(parts[0], parts[2], parts[4], parts[6])
    odd = four(parts[1], parts[3], parts[5], parts[7])
    r = math.sqrt(0.5)
    odd = (
        odd[0],
        ((odd[1][0] + odd[1][1]) * r, (odd[1][1] - odd[1][0]) * r),
        turn(odd[2]),
        ((odd[3][1] - odd[3][0]) * r, -(odd[3][0] + odd[3][1]) * r),
    )
    return [add(e, o) for e, o in zip(even, odd)] + [sub(e, o) for e, o in zip(even, odd)]


def transform(values):
    size = len(values)
    if size == 1:
        return values
    even, odd = transform(values[0::2]), transform(values[1::2])
    first, second = [], []
    for k in range(size // 2):
        (er, ei), (br, bi) = even[k], odd[k]
        if k == 0:
            tr, ti = br, bi
        elif 4 * k == size:
            tr, ti = bi, -br
        else:
            c, s = math.cos(TAU * k / size), -math.sin(TAU * k / size)
            tr, ti = br * c - bi * s, br * s + bi * c
        first.append((er + tr, ei + ti))
        second.append((er - tr, ei - ti))
    return first + second


def real_transform(values):
    size = len(values)
    even, odd = transform(values[0::2]), transform(values[1::2])
    first, second = [], []
    for k in range(size // 2):
        c, s = math.cos(TAU * k / size), -math.sin(TAU * k / size)
        t = odd[k][0] if k == 0 else odd[k][1] if 4 * k == size else odd[k][0] * c - odd[k][1] * s
        first.append(even[k][0] + t)
        second.append(even[k][0] - t)
    return first + second


def across_kernel(
    inner, outer, x_hbm, stage_hbm, u_ref, v_ref, last_ref, out_ref, halo_ref,
    x_ref, stage_ref, parts, rows, send_a, recv_a, send_b, edge,
    sem_x, sem_t, sem_sa, sem_ra, sem_sb, sem_rb, sem_se, sem_re,
):
    devices = inner * outer
    me = lax.axis_index("inner") * outer + lax.axis_index("outer")
    groups, half, _, per, depth, _ = send_a.shape
    side_of = me // half
    place = me % half

    def where(device):
        return (device // outer, device % outer)

    def near(step):
        return side_of * half + (place + step) % half

    def far(step):
        return (1 - side_of) * half + (place + step) % half

    def load_x(part):
        return pltpu.make_async_copy(x_hbm.at[part], x_ref.at[part], sem_x.at[part])

    def load_table(p):
        return pltpu.make_async_copy(stage_hbm.at[p], stage_ref.at[p], sem_t.at[p])

    for part in range(2):
        load_x(part).start()

    @pl.loop(0, RADIX)
    def _(p):
        load_table(p).start()

    barrier = pltpu.get_barrier_semaphore()

    @pl.loop(1, devices)
    def _(step):
        pl.semaphore_signal(barrier, inc=1, device_id=where((me + step) % devices), device_id_type=MESH)

    for part in range(2):
        load_x(part).wait()

    @pl.loop(0, STEPS // 32)
    def _(tile):
        at = pl.ds(pl.multiple_of(tile * 32, 32), 32)
        done = radix_8([(x_ref[0, q, at], x_ref[1, q, at]) for q in range(RADIX)])
        for p in range(RADIX):
            parts[p, at, :LANES] = done[p][0]
            parts[p, at, LANES:] = done[p][1]

    def dot(a, b):
        return jnp.dot(a, b, preferred_element_type=jnp.float32)

    def dot_nt(a, b):
        return lax.dot_general(a, b, NT, preferred_element_type=jnp.float32)

    def copy_a(group, target):
        return pltpu.make_async_remote_copy(
            src_ref=send_a.at[group, target % half], dst_ref=recv_a.at[group, place],
            send_sem=sem_sa.at[group], recv_sem=sem_ra.at[group],
            device_id=where(target), device_id_type=MESH,
        )

    def copy_b(group, target):
        return pltpu.make_async_remote_copy(
            src_ref=send_b.at[group, target], dst_ref=out_ref.at[group, me],
            send_sem=sem_sb.at[group], recv_sem=sem_rb.at[group],
            device_id=where(target), device_id_type=MESH,
        )

    def whole(ref, group, sem_sent, sem_here):
        count = ref.shape[1] - 1
        return pltpu.make_async_remote_copy(
            src_ref=ref.at[group, pl.ds(0, count)], dst_ref=ref.at[group, pl.ds(0, count)],
            send_sem=sem_sent.at[group], recv_sem=sem_here.at[group],
            device_id=where((me + 1) % devices), device_id_type=MESH,
        )

    def copy_edge(target, end, source_side):
        shift = 1 if end else -1
        return pltpu.make_async_remote_copy(
            src_ref=edge.at[target + shift], dst_ref=halo_ref.at[end, side_of],
            send_sem=sem_se.at[target], recv_sem=sem_re.at[end, source_side],
            device_id=where(target), device_id_type=MESH,
        )

    last_high, last_low = halves(last_ref[...])

    def spectrum(group, member):
        p = group * per + member
        load_table(p).wait()
        high, low = halves(parts[p])
        cos_high, cos_low, sin_high, sin_low = (stage_ref[p, i] for i in range(4))
        by_cos = dot(cos_high, high) + dot(cos_high, low) + dot(cos_low, high)
        by_sin = dot(sin_high, high) + dot(sin_high, low) + dot(sin_low, high)
        real = by_cos[:, :LANES] - by_sin[:, LANES:]
        imag = by_cos[:, LANES:] + by_sin[:, :LANES]
        vr, vi = v_ref[0, pl.ds(p, 1)], v_ref[1, pl.ds(p, 1)]
        ur, ui = u_ref[0], u_ref[1]
        tr, ti = ur * vr - ui * vi, ur * vi + ui * vr
        both = jnp.concatenate([real * tr - imag * ti, real * ti + imag * tr], axis=1)
        high, low = halves(both)
        z = dot_nt(last_high, high) + dot_nt(last_high, low) + dot_nt(last_low, high)
        for part in range(2):
            block = z[part * LANES : (part + 1) * LANES]
            for lane_half in range(2):
                rows[part, pl.ds(lane_half, LANES, stride=2), :] = block[:, lane_half * LANES : (lane_half + 1) * LANES]
            send_a[group, :, part, member] = rows[part].reshape(half, depth, LANES)

    def spectra(group):
        @pl.loop(0, per)
        def _(member):
            spectrum(group, member)

        recv_a[group, place] = send_a[group, place]

    spectra(0)
    pl.semaphore_wait(barrier, devices - 1)

    @pl.loop(0, AHEAD)
    def _(group):
        @pl.when(group > 0)
        def _():
            spectra(group)

        @pl.loop(1, half)
        def _(step):
            copy_a(group, near(step)).start()

    sign = (1 - 2 * side_of).astype(jnp.float32)

    shape = (depth, LANES)
    row = lax.broadcasted_iota(jnp.int32, shape, 0) + place * depth
    slot = (row * LANES + lax.broadcasted_iota(jnp.int32, shape, 1)) * GAP
    length = STEPS * LANES * GAP * devices

    def combine(group, member):
        within = (slot + (group * per + member)).astype(jnp.float32) / length

        def weighted(k, value):
            centred = (k / devices - 0.5) + within
            return value * (jnp.exp(RATE * centred * centred) * length**-0.5)

        values = [(recv_a[group, a, 0, member], recv_a[group, a, 1, member]) for a in range(half)]
        for k, done in enumerate(real_transform(values)):
            send_b[group, 2 * k, member] = weighted(2 * k, done)
        turned = []
        for a, (vr, vi) in enumerate(values):
            c, s = math.cos(TAU * a / devices), -math.sin(TAU * a / devices)
            cs, ss = sign * c, sign * s
            turned.append((vr * cs, vi * cs) if a == 0 else (vr * cs - vi * ss, vr * ss + vi * cs))
        for k, done in enumerate(real_transform(turned)):
            send_b[group, 2 * k + 1, member] = weighted(2 * k + 1, done)

    def edges(end):
        row = 0 if end else depth - 1
        shift = 1 if end else -1

        @pl.loop(0, devices)
        def _(k):
            for group in range(groups):
                edge[k, group * per : (group + 1) * per] = send_b[group, k, :, row]

        @pl.loop(0, devices)
        def _(target):
            inside = jnp.logical_and(target + shift >= 0, target + shift < devices)

            @pl.when(jnp.logical_and(inside, target != me))
            def _():
                copy_edge(target, end, side_of).start()

    def edges_sent(end):
        shift = 1 if end else -1

        @pl.loop(0, devices)
        def _(target):
            inside = jnp.logical_and(target + shift >= 0, target + shift < devices)

            @pl.when(jnp.logical_and(inside, target != me))
            def _():
                copy_edge(target, end, side_of).wait_send()

    @pl.loop(0, groups)
    def _(group):
        @pl.when(group + AHEAD < groups)
        def _():
            spectra(group + AHEAD)

        whole(recv_a, group, sem_sa, sem_ra).wait_recv()

        @pl.loop(0, per)
        def _(member):
            combine(group, member)

        @pl.when(group == groups - 1)
        def _():
            for end in range(2):
                @pl.when(place == (0 if end else half - 1))
                def _():
                    edges(end)

        copy_b(group, far(0)).start()

        @pl.loop(1, half)
        def _(step):
            copy_b(group, far(step)).start()
            copy_b(group, near(step)).start()

            @pl.when(group + AHEAD < groups)
            def _():
                copy_a(group + AHEAD, near(step)).start()

        out_ref[group, me] = send_b[group, me]

    for end in range(2):
        sender = 0 if end else half - 1
        bound = devices - 1 if end else 0
        shift = 1 if end else -1

        @pl.when(me == bound)
        def _():
            halo_ref[end] = jnp.zeros(halo_ref.shape[1:], jnp.float32)

        @pl.when(me != bound)
        def _():
            for source_side in range(2):
                source = source_side * half + sender

                @pl.when(me == source)
                def _():
                    halo_ref[end, source_side] = edge[me + shift]

                @pl.when(me != source)
                def _():
                    copy_edge(me, end, source_side).wait_recv()

    @pl.loop(0, groups)
    def _(group):
        whole(out_ref, group, sem_sb, sem_rb).wait_recv()

    for end in range(2):
        @pl.when(place == (0 if end else half - 1))
        def _():
            edges_sent(end)

    @pl.loop(0, groups)
    def _(group):
        whole(send_a, group, sem_sa, sem_ra).wait_send()
        whole(send_b, group, sem_sb, sem_rb).wait_send()


def across(samples, inner, outer):
    devices = inner * outer
    seg = samples.shape[2]
    length = seg * devices
    me = lax.axis_index("inner") * outer + lax.axis_index("outer")
    half = devices // 2
    depth = STEPS // half
    per = RADIX // GROUPS
    x = samples.reshape(2, RADIX, STEPS, LANES)

    def phase(number, order):
        angle = number.astype(jnp.float32) * (-TAU / order)
        return jnp.cos(angle), jnp.sin(angle)

    f = lax.broadcasted_iota(jnp.int32, (STEPS, LANES), 0)
    u = jnp.stack(phase(f * (lax.broadcasted_iota(jnp.int32, (STEPS, LANES), 1) * devices + me), length // RADIX))
    p = lax.broadcasted_iota(jnp.int32, (RADIX, LANES), 0)
    v = jnp.stack(phase(p * (lax.broadcasted_iota(jnp.int32, (RADIX, LANES), 1) * devices + me), length))
    g = lax.broadcasted_iota(jnp.int32, (LANES, LANES), 0)
    order = LANES * devices
    number = g * (lax.broadcasted_iota(jnp.int32, (LANES, LANES), 1) * devices + me) % order
    cosine, sine = phase(number, order)
    last = jnp.concatenate(
        [jnp.concatenate([cosine, -sine], axis=1), jnp.concatenate([sine, cosine], axis=1)], axis=0
    )
    vmem = pl.BlockSpec(memory_space=pltpu.VMEM)
    first = (GROUPS, half, 2, per, depth, LANES)
    block = (GROUPS, devices, per, depth, LANES)
    return pl.pallas_call(
        functools.partial(across_kernel, inner, outer),
        out_shape=(
            jax.ShapeDtypeStruct(block, jnp.float32),
            jax.ShapeDtypeStruct((2, 2, RADIX, LANES), jnp.float32),
        ),
        in_specs=[pl.BlockSpec(memory_space=pltpu.HBM)] * 2 + [vmem] * 3,
        out_specs=(vmem, vmem),
        scratch_shapes=[
            pltpu.VMEM(x.shape, jnp.float32),
            pltpu.VMEM((RADIX, 4, STEPS, STEPS), jnp.bfloat16),
            pltpu.VMEM((RADIX, STEPS, 2 * LANES), jnp.float32),
            pltpu.VMEM((2, STEPS, LANES), jnp.float32),
            pltpu.VMEM(first, jnp.float32),
            pltpu.VMEM(first, jnp.float32),
            pltpu.VMEM(block, jnp.float32),
            pltpu.VMEM((devices, RADIX, LANES), jnp.float32),
        ]
        + [pltpu.SemaphoreType.DMA((2,)), pltpu.SemaphoreType.DMA((RADIX,))]
        + [pltpu.SemaphoreType.DMA((GROUPS,))] * 4
        + [pltpu.SemaphoreType.DMA((devices,)), pltpu.SemaphoreType.DMA((2, 2))],
        compiler_params=pltpu.CompilerParams(
            collective_id=0, has_side_effects=True, vmem_limit_bytes=48 * 2**20
        ),
    )(x, jnp.asarray(stage_table()), u, v, last)


def gram_kernel(inner, outer, real_ref, halo_ref, index_ref, offset_ref, weight_ref, order_ref, z_ref, gram_ref, field):
    devices = inner * outer
    groups, _, per, depth, _ = real_ref.shape
    half = devices // 2

    @pl.loop(0, half)
    def _(e):
        at = pl.ds(pl.multiple_of(8 + e * depth, math.gcd(8, depth)), depth)
        for group in range(groups):
            members = slice(group * per, (group + 1) * per)
            field[members, at, :] = real_ref[group, e] + real_ref[group, half + e]

    halo = halo_ref[:, 0] + halo_ref[:, 1]
    field[:, 7:8, :] = halo[0][:, None, :]
    field[:, STEPS + 8 : STEPS + 9, :] = halo[1][:, None, :]

    lane = lax.broadcasted_iota(jnp.int32, (8, LANES), 1)

    @pl.loop(0, STEPS // 8, unroll=2)
    def _(tile):
        row = pl.multiple_of(tile * 8, 8)
        index = index_ref[pl.ds(row, 8)]
        offset = offset_ref[pl.ds(row, 8)]
        samples = {}
        for p in range(GAP):
            now = field[p, pl.ds(row + 8, 8)]
            before = field[p, pl.ds(row + 7, 8)]
            after = field[p, pl.ds(row + 9, 8)]
            for slot in (-2, -1, 0, 1, 2):
                place = GAP * slot + p
                if place < 1 - HALF or place > HALF + GAP - 1:
                    continue
                if slot < 0:
                    value = pltpu.roll(jnp.where(lane >= LANES + slot, before, now), -slot, 1)
                elif slot > 0:
                    value = pltpu.roll(jnp.where(lane < slot, after, now), LANES - slot, 1)
                else:
                    value = now
                samples[place] = value
        window = [samples[place] for place in range(1 - HALF, HALF + GAP)]
        for bit in (4, 2, 1):
            chosen = (index & bit) != 0
            window = [jnp.where(chosen, b, a) for a, b in zip(window[:-bit], window[bit:])]
        total = jnp.zeros((8, LANES), jnp.float32)
        for tap in range(2 * HALF):
            total += window[tap] * jnp.take_along_axis(weight_ref[tap], offset, axis=1)
        gram_ref[pl.ds(row, 8)] = total

    width = 2 * LANES
    share = width // GAP
    run = lax.broadcasted_iota(jnp.int32, (STEPS, LANES), 1) // share
    for column in range(LANES // share):
        packed = []
        for first in range(0, GAP, LANES // share):
            piece = None
            for place in range(LANES // share):
                value = field[first + place, 8 : STEPS + 8, :]
                turn = (place - column) * share % LANES
                value = pltpu.roll(value, turn, 1) if turn else value
                piece = value if piece is None else jnp.where(run == place, value, piece)
            packed.append(piece)
        rest = jnp.concatenate(packed, axis=1)
        block = None
        for _ in range(3):
            piece = rest.astype(jnp.bfloat16)
            rest = rest - piece.astype(jnp.float32)
            product = jnp.dot(piece, order_ref[...], preferred_element_type=jnp.float32)
            block = product if block is None else block + product
        for side in range(2):
            z_ref[pl.ds(2 * column + side, STEPS, stride=GAP), :] = block[:, side * LANES : (side + 1) * LANES]


def local(inner, outer, samples, gram_index, gram_offset):
    real, halo = across(samples, inner, outer)
    rows = (STEPS, LANES)
    z, gram = pl.pallas_call(
        functools.partial(gram_kernel, inner, outer),
        out_shape=(
            jax.ShapeDtypeStruct((STEPS * GAP, LANES), jnp.float32),
            jax.ShapeDtypeStruct(rows, jnp.float32),
        ),
        in_specs=[pl.BlockSpec(memory_space=pltpu.VMEM)] * 6,
        out_specs=(pl.BlockSpec(memory_space=pltpu.VMEM),) * 2,
        scratch_shapes=[pltpu.VMEM((GAP, STEPS + 16, LANES), jnp.float32)],
        compiler_params=pltpu.CompilerParams(vmem_limit_bytes=48 * 2**20),
    )(
        real, halo, gram_index.reshape(rows), gram_offset.reshape(rows),
        jnp.asarray(weight_table()), jnp.asarray(order_table()),
    )
    return z.reshape(-1), gram.reshape(-1)


def solution(mesh):
    return jax.shard_map(
        functools.partial(local, mesh.shape["inner"], mesh.shape["outer"]),
        mesh=mesh,
        in_specs=(P(None, ("inner", "outer"), None), P(("inner", "outer")), P(("inner", "outer"))),
        out_specs=(P(("inner", "outer")), P(("inner", "outer"))),
        check_vma=False,
    )
```

```python
import functools
import math

import jax
import jax.numpy as jnp
import numpy as np
from jax import lax
from jax.experimental import pallas as pl
from jax.experimental.pallas import tpu as pltpu
from jax.sharding import PartitionSpec as P

GAP = 8
HALF = 16
UPS = 32
LANES = 128
RADIX = 8
STEPS = 256
GROUPS = 8
TAU = 2.0 * math.pi
RATE = 4.0
MESH = pl.DeviceIdType.MESH
NT = (((1,), (1,)), ((), ()))


def halves(x):
    high = x.astype(jnp.bfloat16)
    low = (x - high.astype(jnp.float32)).astype(jnp.bfloat16)
    return high, low


def np_halves(x):
    x = x.astype(np.float32)
    high = x.astype(jnp.bfloat16)
    low = (x - high.astype(np.float32)).astype(jnp.bfloat16)
    return high, low


def stage_table():
    p = np.arange(RADIX)[:, None, None]
    f = np.arange(STEPS)[None, :, None]
    t = np.arange(STEPS)[None, None, :]
    order = RADIX * STEPS
    angle = (t * (RADIX * f + p) % order) * (-TAU / order)
    return np.stack([*np_halves(np.cos(angle)), *np_halves(np.sin(angle))], axis=1)


def order_table():
    size = 2 * LANES
    p, l = np.divmod(np.arange(size), size // GAP)
    table = np.zeros((size, size), np.float32)
    table[np.arange(size), GAP * l + p] = 1.0
    return table.astype(jnp.bfloat16)


def weight_table():
    tap = np.arange(1 - HALF, HALF + 1)[:, None]
    distance = np.arange(LANES)[None, :] % UPS / UPS - tap
    spread = HALF / 2.0
    table = np.sinc(distance) * np.exp(-distance * distance / (2.0 * spread * spread))
    return np.broadcast_to(table.astype(np.float32)[:, None, :], (2 * HALF, 8, LANES)).copy()


def radix_8(parts):
    def add(u, v):
        return u[0] + v[0], u[1] + v[1]

    def sub(u, v):
        return u[0] - v[0], u[1] - v[1]

    def turn(u):
        return u[1], -u[0]

    def four(a, b, c, d):
        s, t, u, v = add(a, c), sub(a, c), add(b, d), turn(sub(b, d))
        return add(s, u), add(t, v), sub(s, u), sub(t, v)

    even = four(parts[0], parts[2], parts[4], parts[6])
    odd = four(parts[1], parts[3], parts[5], parts[7])
    r = math.sqrt(0.5)
    odd = (
        odd[0],
        ((odd[1][0] + odd[1][1]) * r, (odd[1][1] - odd[1][0]) * r),
        turn(odd[2]),
        ((odd[3][1] - odd[3][0]) * r, -(odd[3][0] + odd[3][1]) * r),
    )
    return [add(e, o) for e, o in zip(even, odd)] + [sub(e, o) for e, o in zip(even, odd)]


def transform(values):
    size = len(values)
    if size == 1:
        return values
    even, odd = transform(values[0::2]), transform(values[1::2])
    first, second = [], []
    for k in range(size // 2):
        (er, ei), (br, bi) = even[k], odd[k]
        if k == 0:
            tr, ti = br, bi
        elif 4 * k == size:
            tr, ti = bi, -br
        else:
            c, s = math.cos(TAU * k / size), -math.sin(TAU * k / size)
            tr, ti = br * c - bi * s, br * s + bi * c
        first.append((er + tr, ei + ti))
        second.append((er - tr, ei - ti))
    return first + second


def real_transform(values):
    size = len(values)
    even, odd = transform(values[0::2]), transform(values[1::2])
    first, second = [], []
    for k in range(size // 2):
        c, s = math.cos(TAU * k / size), -math.sin(TAU * k / size)
        t = odd[k][0] if k == 0 else odd[k][1] if 4 * k == size else odd[k][0] * c - odd[k][1] * s
        first.append(even[k][0] + t)
        second.append(even[k][0] - t)
    return first + second


def across_kernel(
    inner, outer, x_hbm, stage_hbm, u_ref, v_ref, last_ref, out_ref, halo_ref,
    x_ref, stage_ref, parts, rows, send_a, recv_a, raw, own, both, arrived, total, edge,
    sem_x, sem_t, sem_sa, sem_ra, sem_sw, sem_rw, sem_sp, sem_rp, sem_sb, sem_rb, sem_se, sem_re,
):
    devices = inner * outer
    me = lax.axis_index("inner") * outer + lax.axis_index("outer")
    groups, quarter, _, per, depth, _ = send_a.shape
    plane = me // quarter
    place = me % quarter
    near_plane = plane + 1 - 2 * (plane % 2)
    far_plane = 3 - plane
    far_outer = far_plane + 1 - 2 * (far_plane % 2)
    is_outer = jnp.logical_or(plane == 0, plane == 3)
    is_inner = jnp.logical_not(is_outer)

    def where(device):
        return (device // outer, device % outer)

    def beside(step):
        return plane * quarter + (place + step) % quarter

    def load_x(part):
        return pltpu.make_async_copy(x_hbm.at[part], x_ref.at[part], sem_x.at[part])

    def load_table(p):
        return pltpu.make_async_copy(stage_hbm.at[p], stage_ref.at[p], sem_t.at[p])

    for part in range(2):
        load_x(part).start()

    @pl.loop(0, RADIX)
    def _(p):
        load_table(p).start()

    barrier = pltpu.get_barrier_semaphore()

    @pl.loop(1, devices)
    def _(step):
        pl.semaphore_signal(barrier, inc=1, device_id=where((me + step) % devices), device_id_type=MESH)

    for part in range(2):
        load_x(part).wait()

    @pl.loop(0, STEPS // 32)
    def _(tile):
        at = pl.ds(pl.multiple_of(tile * 32, 32), 32)
        done = radix_8([(x_ref[0, q, at], x_ref[1, q, at]) for q in range(RADIX)])
        for p in range(RADIX):
            parts[p, at, :LANES] = done[p][0]
            parts[p, at, LANES:] = done[p][1]

    def dot(a, b):
        return jnp.dot(a, b, preferred_element_type=jnp.float32)

    def dot_nt(a, b):
        return lax.dot_general(a, b, NT, preferred_element_type=jnp.float32)

    def send(source, target_ref, sent, here, device):
        return pltpu.make_async_remote_copy(
            src_ref=source, dst_ref=target_ref, send_sem=sent, recv_sem=here,
            device_id=where(device), device_id_type=MESH,
        )

    def copy_a(group, target):
        return send(
            send_a.at[group, target % quarter], recv_a.at[group, place], sem_sa.at[group], sem_ra.at[group], target
        )

    def copy_b(group, target):
        return send(
            total.at[group, target % quarter], out_ref.at[group, place], sem_sb.at[group], sem_rb.at[group], target
        )

    def copy_raw(group):
        return send(
            recv_a.at[group], raw.at[group], sem_sw.at[group], sem_rw.at[group], near_plane * quarter + place
        )

    def copy_part(source, group, slot, number, to_plane):
        return send(
            source.at[group, pl.ds(to_plane * quarter, quarter)], arrived.at[group, slot],
            sem_sp.at[group, number], sem_rp.at[group, slot], to_plane * quarter + place,
        )

    def copy_far(group):
        return copy_part(both, group, 0, 0, far_plane)

    def copy_far_outer(group):
        return copy_part(both, group, 0, 1, far_outer)

    def copy_near(group):
        return copy_part(own, group, 1, 2, near_plane)

    def whole(ref, group, sem_sent, sem_here):
        part = ref.at[group, pl.ds(0, quarter - 1)]
        return send(part, part, sem_sent.at[group], sem_here.at[group], beside(1))

    def copy_edge(kk, end):
        target = (plane * quarter + kk - (1 if end else -1) + devices) % devices
        return send(edge.at[kk], halo_ref.at[end], sem_se.at[kk], sem_re.at[end], target)

    last_high, last_low = halves(last_ref[...])

    def spectrum(group, member):
        p = group * per + member
        load_table(p).wait()
        high, low = halves(parts[p])
        cos_high, cos_low, sin_high, sin_low = (stage_ref[p, i] for i in range(4))
        by_cos = dot(cos_high, high) + dot(cos_high, low) + dot(cos_low, high)
        by_sin = dot(sin_high, high) + dot(sin_high, low) + dot(sin_low, high)
        real = by_cos[:, :LANES] - by_sin[:, LANES:]
        imag = by_cos[:, LANES:] + by_sin[:, :LANES]
        vr, vi = v_ref[0, pl.ds(p, 1)], v_ref[1, pl.ds(p, 1)]
        ur, ui = u_ref[0], u_ref[1]
        tr, ti = ur * vr - ui * vi, ur * vi + ui * vr
        both = jnp.concatenate([real * tr - imag * ti, real * ti + imag * tr], axis=1)
        high, low = halves(both)
        z = dot_nt(last_high, high) + dot_nt(last_high, low) + dot_nt(last_low, high)
        for part in range(2):
            block = z[part * LANES : (part + 1) * LANES]
            for lane_half in range(2):
                rows[part, pl.ds(lane_half, LANES, stride=2), :] = block[:, lane_half * LANES : (lane_half + 1) * LANES]
            send_a[group, :, part, member] = rows[part].reshape(quarter, depth, LANES)

    def spectra(group):
        @pl.loop(0, per)
        def _(member):
            spectrum(group, member)

        recv_a[group, place] = send_a[group, place]

    def factors(which):
        pairs = []
        for v in range(4):
            turns = (which * v) % 4
            real = jnp.where(turns == 0, 1.0, jnp.where(turns == 2, -1.0, 0.0))
            imag = jnp.where(turns == 1, -1.0, jnp.where(turns == 3, 1.0, 0.0))
            pairs.append((real, imag))
        return pairs

    def outputs(values, pairs):
        result = [None] * devices
        for v in range(4):
            turned = []
            for a, (vr, vi) in enumerate(values):
                c, s = math.cos(TAU * a * v / devices), -math.sin(TAU * a * v / devices)
                turned.append((vr, vi) if a * v == 0 else (vr * c - vi * s, vr * s + vi * c))
            for u, (real, imag) in enumerate(transform(turned)):
                result[4 * u + v] = real if v == 0 else real * pairs[v][0] - imag * pairs[v][1]
        return result

    tall = min(8, depth)

    def tiles(body):
        @pl.loop(0, per)
        def _(member):
            @pl.loop(0, depth // tall)
            def _(tile):
                body(member, pl.ds(pl.multiple_of(tile * tall, tall), tall), tile * tall)

    own_pairs, near_pairs = factors(plane), factors(near_plane)

    def first_stage(group):
        spectra(group)

        @pl.when(group == 0)
        def _():
            pl.semaphore_wait(barrier, devices - 1)

        @pl.loop(1, quarter)
        def _(step):
            copy_a(group, beside(step)).start()

    def second_stage(group):
        whole(recv_a, group, sem_sa, sem_ra).wait_recv()

        @pl.when(is_outer)
        def _():
            copy_raw(group).start()

        def body(member, at, first):
            values = [(recv_a[group, a, 0, member, at], recv_a[group, a, 1, member, at]) for a in range(quarter)]
            for k, done in enumerate(outputs(values, own_pairs)):
                own[group, k, member, at] = done

        tiles(body)

        @pl.when(is_inner)
        def _():
            copy_near(group).start()

    def third_stage(group):
        @pl.when(is_inner)
        def _():
            copy_raw(group).wait_recv()

            def body(member, at, first):
                values = [(raw[group, a, 0, member, at], raw[group, a, 1, member, at]) for a in range(quarter)]
                for k, done in enumerate(outputs(values, near_pairs)):
                    both[group, k, member, at] = done + own[group, k, member, at]

            tiles(body)
            copy_far(group).start()
            copy_far_outer(group).start()

    length = STEPS * LANES * GAP * devices
    lanes = lax.broadcasted_iota(jnp.int32, (tall, LANES), 1)
    lines = lax.broadcasted_iota(jnp.int32, (tall, LANES), 0)
    base = plane.astype(jnp.float32) * 0.25 - 0.5

    def finish(group, gather):
        def body(member, at, first):
            slot = ((lines + (place * depth + first)) * LANES + lanes) * GAP
            within = (slot + (group * per + member)).astype(jnp.float32) / length
            for kk in range(quarter):
                centred = (base + kk / devices) + within
                weight = jnp.exp(RATE * centred * centred) * length**-0.5
                total[group, kk, member, at] = gather(kk, member, at) * weight

        tiles(body)

    def edges(end):
        row = 0 if end else depth - 1
        shift = 1 if end else -1

        @pl.loop(0, quarter)
        def _(kk):
            for group in range(groups):
                edge[kk, group * per : (group + 1) * per] = total[group, kk, :, row]

        @pl.loop(0, quarter)
        def _(kk):
            target = plane * quarter + kk - shift
            inside = jnp.logical_and(target >= 0, target < devices)

            @pl.when(jnp.logical_and(inside, target != me))
            def _():
                copy_edge(kk, end).start()

    def edges_sent(end):
        shift = 1 if end else -1

        @pl.loop(0, quarter)
        def _(kk):
            target = plane * quarter + kk - shift
            inside = jnp.logical_and(target >= 0, target < devices)

            @pl.when(jnp.logical_and(inside, target != me))
            def _():
                copy_edge(kk, end).wait_send()

    def last_stage(group):
        copy_far(group).wait_recv()

        @pl.when(is_outer)
        def _():
            copy_near(group).wait_recv()
            finish(
                group,
                lambda kk, member, at: own[group, plane * quarter + kk, member, at]
                + (arrived[group, 1, kk, member, at] + arrived[group, 0, kk, member, at]),
            )

        @pl.when(is_inner)
        def _():
            finish(
                group,
                lambda kk, member, at: both[group, plane * quarter + kk, member, at] + arrived[group, 0, kk, member, at],
            )

        @pl.when(group == groups - 1)
        def _():
            for end in range(2):
                @pl.when(place == (0 if end else quarter - 1))
                def _():
                    edges(end)

        @pl.loop(1, quarter)
        def _(step):
            copy_b(group, beside(step)).start()

        out_ref[group, place] = total[group, place]

    stages = (first_stage, second_stage, third_stage, last_stage)

    @pl.loop(0, groups + len(stages) - 1)
    def _(turn):
        for lag, stage in enumerate(stages):
            @pl.when(jnp.logical_and(turn >= lag, turn < groups + lag))
            def _():
                stage(turn - lag)

    for end in range(2):
        sender = 0 if end else quarter - 1
        bound = devices - 1 if end else 0

        @pl.when(me == bound)
        def _():
            halo_ref[end] = jnp.zeros(halo_ref.shape[1:], jnp.float32)

        @pl.when(jnp.logical_and(me != bound, place == sender))
        def _():
            halo_ref[end] = edge[sender + (1 if end else -1)]

        @pl.when(jnp.logical_and(me != bound, place != sender))
        def _():
            copy_edge(0, end).wait_recv()

    @pl.loop(0, groups)
    def _(group):
        whole(out_ref, group, sem_sb, sem_rb).wait_recv()

    for end in range(2):
        @pl.when(place == (0 if end else quarter - 1))
        def _():
            edges_sent(end)

    @pl.loop(0, groups)
    def _(group):
        whole(send_a, group, sem_sa, sem_ra).wait_send()
        whole(total, group, sem_sb, sem_rb).wait_send()

        @pl.when(is_outer)
        def _():
            copy_raw(group).wait_send()

        @pl.when(is_inner)
        def _():
            copy_far(group).wait_send()
            copy_far_outer(group).wait_send()
            copy_near(group).wait_send()


def across(samples, inner, outer):
    devices = inner * outer
    seg = samples.shape[2]
    length = seg * devices
    me = lax.axis_index("inner") * outer + lax.axis_index("outer")
    quarter = devices // 4
    depth = STEPS // quarter
    per = RADIX // GROUPS
    x = samples.reshape(2, RADIX, STEPS, LANES)

    def phase(number, order):
        angle = number.astype(jnp.float32) * (-TAU / order)
        return jnp.cos(angle), jnp.sin(angle)

    f = lax.broadcasted_iota(jnp.int32, (STEPS, LANES), 0)
    u = jnp.stack(phase(f * (lax.broadcasted_iota(jnp.int32, (STEPS, LANES), 1) * devices + me), length // RADIX))
    p = lax.broadcasted_iota(jnp.int32, (RADIX, LANES), 0)
    v = jnp.stack(phase(p * (lax.broadcasted_iota(jnp.int32, (RADIX, LANES), 1) * devices + me), length))
    g = lax.broadcasted_iota(jnp.int32, (LANES, LANES), 0)
    order = LANES * devices
    number = g * (lax.broadcasted_iota(jnp.int32, (LANES, LANES), 1) * devices + me) % order
    cosine, sine = phase(number, order)
    last = jnp.concatenate(
        [jnp.concatenate([cosine, -sine], axis=1), jnp.concatenate([sine, cosine], axis=1)], axis=0
    )
    vmem = pl.BlockSpec(memory_space=pltpu.VMEM)
    first = (GROUPS, quarter, 2, per, depth, LANES)
    block = (GROUPS, quarter, per, depth, LANES)
    wide = (GROUPS, devices, per, depth, LANES)
    return pl.pallas_call(
        functools.partial(across_kernel, inner, outer),
        out_shape=(
            jax.ShapeDtypeStruct(block, jnp.float32),
            jax.ShapeDtypeStruct((2, RADIX, LANES), jnp.float32),
        ),
        in_specs=[pl.BlockSpec(memory_space=pltpu.HBM)] * 2 + [vmem] * 3,
        out_specs=(vmem, vmem),
        scratch_shapes=[
            pltpu.VMEM(x.shape, jnp.float32),
            pltpu.VMEM((RADIX, 4, STEPS, STEPS), jnp.bfloat16),
            pltpu.VMEM((RADIX, STEPS, 2 * LANES), jnp.float32),
            pltpu.VMEM((2, STEPS, LANES), jnp.float32),
            pltpu.VMEM(first, jnp.float32),
            pltpu.VMEM(first, jnp.float32),
            pltpu.VMEM(first, jnp.float32),
            pltpu.VMEM(wide, jnp.float32),
            pltpu.VMEM(wide, jnp.float32),
            pltpu.VMEM((GROUPS, 2, quarter, per, depth, LANES), jnp.float32),
            pltpu.VMEM(block, jnp.float32),
            pltpu.VMEM((quarter, RADIX, LANES), jnp.float32),
        ]
        + [pltpu.SemaphoreType.DMA((2,)), pltpu.SemaphoreType.DMA((RADIX,))]
        + [pltpu.SemaphoreType.DMA((GROUPS,))] * 4
        + [pltpu.SemaphoreType.DMA((GROUPS, 3)), pltpu.SemaphoreType.DMA((GROUPS, 2))]
        + [pltpu.SemaphoreType.DMA((GROUPS,))] * 2
        + [pltpu.SemaphoreType.DMA((quarter,)), pltpu.SemaphoreType.DMA((2,))],
        compiler_params=pltpu.CompilerParams(
            collective_id=0, has_side_effects=True, vmem_limit_bytes=48 * 2**20
        ),
    )(x, jnp.asarray(stage_table()), u, v, last)


def gram_kernel(inner, outer, real_ref, halo_ref, index_ref, offset_ref, weight_ref, order_ref, z_ref, gram_ref, field):
    devices = inner * outer
    groups, _, per, depth, _ = real_ref.shape

    @pl.loop(0, devices // 4)
    def _(e):
        at = pl.ds(pl.multiple_of(8 + e * depth, math.gcd(8, depth)), depth)
        for group in range(groups):
            field[group * per : (group + 1) * per, at, :] = real_ref[group, e]

    field[:, 7:8, :] = halo_ref[0][:, None, :]
    field[:, STEPS + 8 : STEPS + 9, :] = halo_ref[1][:, None, :]

    lane = lax.broadcasted_iota(jnp.int32, (8, LANES), 1)

    @pl.loop(0, STEPS // 8, unroll=2)
    def _(tile):
        row = pl.multiple_of(tile * 8, 8)
        index = index_ref[pl.ds(row, 8)]
        offset = offset_ref[pl.ds(row, 8)]
        samples = {}
        for p in range(GAP):
            now = field[p, pl.ds(row + 8, 8)]
            before = field[p, pl.ds(row + 7, 8)]
            after = field[p, pl.ds(row + 9, 8)]
            for slot in (-2, -1, 0, 1, 2):
                place = GAP * slot + p
                if place < 1 - HALF or place > HALF + GAP - 1:
                    continue
                if slot < 0:
                    value = pltpu.roll(jnp.where(lane >= LANES + slot, before, now), -slot, 1)
                elif slot > 0:
                    value = pltpu.roll(jnp.where(lane < slot, after, now), LANES - slot, 1)
                else:
                    value = now
                samples[place] = value
        window = [samples[place] for place in range(1 - HALF, HALF + GAP)]
        for bit in (4, 2, 1):
            chosen = (index & bit) != 0
            window = [jnp.where(chosen, b, a) for a, b in zip(window[:-bit], window[bit:])]
        total = jnp.zeros((8, LANES), jnp.float32)
        for tap in range(2 * HALF):
            total += window[tap] * jnp.take_along_axis(weight_ref[tap], offset, axis=1)
        gram_ref[pl.ds(row, 8)] = total

    width = 2 * LANES
    share = width // GAP
    run = lax.broadcasted_iota(jnp.int32, (STEPS, LANES), 1) // share
    for column in range(LANES // share):
        packed = []
        for first in range(0, GAP, LANES // share):
            piece = None
            for place in range(LANES // share):
                value = field[first + place, 8 : STEPS + 8, :]
                turn = (place - column) * share % LANES
                value = pltpu.roll(value, turn, 1) if turn else value
                piece = value if piece is None else jnp.where(run == place, value, piece)
            packed.append(piece)
        rest = jnp.concatenate(packed, axis=1)
        block = None
        for _ in range(3):
            piece = rest.astype(jnp.bfloat16)
            rest = rest - piece.astype(jnp.float32)
            product = jnp.dot(piece, order_ref[...], preferred_element_type=jnp.float32)
            block = product if block is None else block + product
        for side in range(2):
            z_ref[pl.ds(2 * column + side, STEPS, stride=GAP), :] = block[:, side * LANES : (side + 1) * LANES]


def local(inner, outer, samples, gram_index, gram_offset):
    real, halo = across(samples, inner, outer)
    rows = (STEPS, LANES)
    z, gram = pl.pallas_call(
        functools.partial(gram_kernel, inner, outer),
        out_shape=(
            jax.ShapeDtypeStruct((STEPS * GAP, LANES), jnp.float32),
            jax.ShapeDtypeStruct(rows, jnp.float32),
        ),
        in_specs=[pl.BlockSpec(memory_space=pltpu.VMEM)] * 6,
        out_specs=(pl.BlockSpec(memory_space=pltpu.VMEM),) * 2,
        scratch_shapes=[pltpu.VMEM((GAP, STEPS + 16, LANES), jnp.float32)],
        compiler_params=pltpu.CompilerParams(vmem_limit_bytes=48 * 2**20),
    )(
        real, halo, gram_index.reshape(rows), gram_offset.reshape(rows),
        jnp.asarray(weight_table()), jnp.asarray(order_table()),
    )
    return z.reshape(-1), gram.reshape(-1)


def solution(mesh):
    return jax.shard_map(
        functools.partial(local, mesh.shape["inner"], mesh.shape["outer"]),
        mesh=mesh,
        in_specs=(P(None, ("inner", "outer"), None), P(("inner", "outer")), P(("inner", "outer"))),
        out_specs=(P(("inner", "outer")), P(("inner", "outer"))),
        check_vma=False,
    )
```

```python
import functools
import math

import jax
import jax.numpy as jnp
import numpy as np
from jax import lax
from jax.experimental import pallas as pl
from jax.experimental.pallas import tpu as pltpu
from jax.sharding import PartitionSpec as P

GAP = 8
HALF = 16
UPS = 32
LANES = 128
RADIX = 8
STEPS = 256
SPLIT = 2
GROUPS = RADIX * SPLIT
TAU = 2.0 * math.pi
RATE = 4.0
MESH = pl.DeviceIdType.MESH
NT = (((1,), (1,)), ((), ()))


def halves(x):
    high = x.astype(jnp.bfloat16)
    low = (x - high.astype(jnp.float32)).astype(jnp.bfloat16)
    return high, low


def np_halves(x):
    x = x.astype(np.float32)
    high = x.astype(jnp.bfloat16)
    low = (x - high.astype(np.float32)).astype(jnp.bfloat16)
    return high, low


def stage_table():
    p = np.arange(RADIX)[:, None, None]
    f = np.arange(STEPS)[None, :, None]
    t = np.arange(STEPS)[None, None, :]
    order = RADIX * STEPS
    angle = (t * (RADIX * f + p) % order) * (-TAU / order)
    return np.stack([*np_halves(np.cos(angle)), *np_halves(np.sin(angle))], axis=1)


def order_table():
    size = 2 * LANES
    p, l = np.divmod(np.arange(size), size // GAP)
    table = np.zeros((size, size), np.float32)
    table[np.arange(size), GAP * l + p] = 1.0
    return table.astype(jnp.bfloat16)


def weight_table():
    tap = np.arange(1 - HALF, HALF + 1)[:, None]
    distance = np.arange(LANES)[None, :] % UPS / UPS - tap
    spread = HALF / 2.0
    table = np.sinc(distance) * np.exp(-distance * distance / (2.0 * spread * spread))
    return np.broadcast_to(table.astype(np.float32)[:, None, :], (2 * HALF, 8, LANES)).copy()


def radix_8(parts):
    def add(u, v):
        return u[0] + v[0], u[1] + v[1]

    def sub(u, v):
        return u[0] - v[0], u[1] - v[1]

    def turn(u):
        return u[1], -u[0]

    def four(a, b, c, d):
        s, t, u, v = add(a, c), sub(a, c), add(b, d), turn(sub(b, d))
        return add(s, u), add(t, v), sub(s, u), sub(t, v)

    even = four(parts[0], parts[2], parts[4], parts[6])
    odd = four(parts[1], parts[3], parts[5], parts[7])
    r = math.sqrt(0.5)
    odd = (
        odd[0],
        ((odd[1][0] + odd[1][1]) * r, (odd[1][1] - odd[1][0]) * r),
        turn(odd[2]),
        ((odd[3][1] - odd[3][0]) * r, -(odd[3][0] + odd[3][1]) * r),
    )
    return [add(e, o) for e, o in zip(even, odd)] + [sub(e, o) for e, o in zip(even, odd)]


def transform(values):
    size = len(values)
    if size == 1:
        return values
    even, odd = transform(values[0::2]), transform(values[1::2])
    first, second = [], []
    for k in range(size // 2):
        (er, ei), (br, bi) = even[k], odd[k]
        if k == 0:
            tr, ti = br, bi
        elif 4 * k == size:
            tr, ti = bi, -br
        else:
            c, s = math.cos(TAU * k / size), -math.sin(TAU * k / size)
            tr, ti = br * c - bi * s, br * s + bi * c
        first.append((er + tr, ei + ti))
        second.append((er - tr, ei - ti))
    return first + second


def real_transform(values):
    size = len(values)
    even, odd = transform(values[0::2]), transform(values[1::2])
    first, second = [], []
    for k in range(size // 2):
        c, s = math.cos(TAU * k / size), -math.sin(TAU * k / size)
        t = odd[k][0] if k == 0 else odd[k][1] if 4 * k == size else odd[k][0] * c - odd[k][1] * s
        first.append(even[k][0] + t)
        second.append(even[k][0] - t)
    return first + second


def across_kernel(
    inner, outer, x_hbm, stage_hbm, u_ref, v_ref, last_ref, out_ref, halo_ref,
    x_ref, stage_ref, parts, rows, send_a, recv_a, raw, own, both, arrived, total, edge,
    sem_x, sem_t, sem_sa, sem_ra, sem_sw, sem_rw, sem_sp, sem_rp, sem_sb, sem_rb, sem_se, sem_re,
):
    devices = inner * outer
    me = lax.axis_index("inner") * outer + lax.axis_index("outer")
    groups, quarter, _, per, depth, _ = send_a.shape
    plane = me // quarter
    place = me % quarter
    near_plane = plane + 1 - 2 * (plane % 2)
    far_plane = 3 - plane
    far_outer = far_plane + 1 - 2 * (far_plane % 2)
    is_outer = jnp.logical_or(plane == 0, plane == 3)
    is_inner = jnp.logical_not(is_outer)

    def where(device):
        return (device // outer, device % outer)

    def beside(step):
        return plane * quarter + (place + step) % quarter

    def load_x(part):
        return pltpu.make_async_copy(x_hbm.at[part], x_ref.at[part], sem_x.at[part])

    def load_table(p):
        return pltpu.make_async_copy(stage_hbm.at[p], stage_ref.at[p], sem_t.at[p])

    for part in range(2):
        load_x(part).start()

    @pl.loop(0, RADIX)
    def _(p):
        load_table(p).start()

    barrier = pltpu.get_barrier_semaphore()

    @pl.loop(1, devices)
    def _(step):
        pl.semaphore_signal(barrier, inc=1, device_id=where((me + step) % devices), device_id_type=MESH)

    for part in range(2):
        load_x(part).wait()

    @pl.loop(0, STEPS // 32)
    def _(tile):
        at = pl.ds(pl.multiple_of(tile * 32, 32), 32)
        done = radix_8([(x_ref[0, q, at], x_ref[1, q, at]) for q in range(RADIX)])
        for p in range(RADIX):
            parts[p, at, :LANES] = done[p][0]
            parts[p, at, LANES:] = done[p][1]

    def dot(a, b):
        return jnp.dot(a, b, preferred_element_type=jnp.float32)

    def dot_nt(a, b):
        return lax.dot_general(a, b, NT, preferred_element_type=jnp.float32)

    def send(source, target_ref, sent, here, device):
        return pltpu.make_async_remote_copy(
            src_ref=source, dst_ref=target_ref, send_sem=sent, recv_sem=here,
            device_id=where(device), device_id_type=MESH,
        )

    def copy_a(group, target):
        return send(
            send_a.at[group, target % quarter], recv_a.at[group, place], sem_sa.at[group], sem_ra.at[group], target
        )

    def copy_b(group, target):
        return send(
            total.at[group, target % quarter], out_ref.at[group, place], sem_sb.at[group], sem_rb.at[group], target
        )

    def copy_raw(group):
        return send(
            recv_a.at[group], raw.at[group], sem_sw.at[group], sem_rw.at[group], near_plane * quarter + place
        )

    def copy_part(source, group, slot, number, to_plane):
        return send(
            source.at[group, pl.ds(to_plane * quarter, quarter)], arrived.at[group, slot],
            sem_sp.at[group, number], sem_rp.at[group, slot], to_plane * quarter + place,
        )

    def copy_far(group):
        return copy_part(both, group, 0, 0, far_plane)

    def copy_far_outer(group):
        return copy_part(both, group, 0, 1, far_outer)

    def copy_near(group):
        return copy_part(own, group, 1, 2, near_plane)

    def whole(ref, group, sem_sent, sem_here):
        part = ref.at[group, pl.ds(0, quarter - 1)]
        return send(part, part, sem_sent.at[group], sem_here.at[group], beside(1))

    def copy_edge(kk, end):
        target = (plane * quarter + kk - (1 if end else -1) + devices) % devices
        return send(edge.at[kk], halo_ref.at[end], sem_se.at[kk], sem_re.at[end], target)

    last_high, last_low = halves(last_ref[...])

    def spectrum(p):
        load_table(p).wait()
        high, low = halves(parts[p])
        cos_high, cos_low, sin_high, sin_low = (stage_ref[p, i] for i in range(4))
        by_cos = dot(cos_high, high) + dot(cos_high, low) + dot(cos_low, high)
        by_sin = dot(sin_high, high) + dot(sin_high, low) + dot(sin_low, high)
        real = by_cos[:, :LANES] - by_sin[:, LANES:]
        imag = by_cos[:, LANES:] + by_sin[:, :LANES]
        vr, vi = v_ref[0, pl.ds(p, 1)], v_ref[1, pl.ds(p, 1)]
        ur, ui = u_ref[0], u_ref[1]
        tr, ti = ur * vr - ui * vi, ur * vi + ui * vr
        both = jnp.concatenate([real * tr - imag * ti, real * ti + imag * tr], axis=1)
        high, low = halves(both)
        z = dot_nt(last_high, high) + dot_nt(last_high, low) + dot_nt(last_low, high)
        for part in range(2):
            block = z[part * LANES : (part + 1) * LANES]
            for lane_half in range(2):
                rows[part, pl.ds(lane_half, LANES, stride=2), :] = block[:, lane_half * LANES : (lane_half + 1) * LANES]
            value = rows[part].reshape(quarter, SPLIT, depth, LANES)
            for share in range(SPLIT):
                send_a[p * SPLIT + share, :, part, 0] = value[:, share]

    def spectra(group):
        @pl.when(group % SPLIT == 0)
        def _():
            spectrum(group // SPLIT)

        recv_a[group, place] = send_a[group, place]

    def factors(which):
        pairs = []
        for v in range(4):
            turns = (which * v) % 4
            real = jnp.where(turns == 0, 1.0, jnp.where(turns == 2, -1.0, 0.0))
            imag = jnp.where(turns == 1, -1.0, jnp.where(turns == 3, 1.0, 0.0))
            pairs.append((real, imag))
        return pairs

    def outputs(values, pairs):
        result = [None] * devices
        for v in range(4):
            turned = []
            for a, (vr, vi) in enumerate(values):
                c, s = math.cos(TAU * a * v / devices), -math.sin(TAU * a * v / devices)
                turned.append((vr, vi) if a * v == 0 else (vr * c - vi * s, vr * s + vi * c))
            for u, (real, imag) in enumerate(transform(turned)):
                result[4 * u + v] = real if v == 0 else real * pairs[v][0] - imag * pairs[v][1]
        return result

    tall = min(8, depth)

    def tiles(body):
        @pl.loop(0, per)
        def _(member):
            @pl.loop(0, depth // tall)
            def _(tile):
                body(member, pl.ds(pl.multiple_of(tile * tall, tall), tall), tile * tall)

    own_pairs, near_pairs = factors(plane), factors(near_plane)

    def first_stage(group):
        spectra(group)

        @pl.when(group == 0)
        def _():
            pl.semaphore_wait(barrier, devices - 1)

        @pl.loop(1, quarter)
        def _(step):
            copy_a(group, beside(step)).start()

    def second_stage(group):
        whole(recv_a, group, sem_sa, sem_ra).wait_recv()

        @pl.when(is_outer)
        def _():
            copy_raw(group).start()

        def body(member, at, first):
            values = [(recv_a[group, a, 0, member, at], recv_a[group, a, 1, member, at]) for a in range(quarter)]
            for k, done in enumerate(outputs(values, own_pairs)):
                own[group, k, member, at] = done

        tiles(body)

        @pl.when(is_inner)
        def _():
            copy_near(group).start()

    def third_stage(group):
        @pl.when(is_inner)
        def _():
            copy_raw(group).wait_recv()

            def body(member, at, first):
                values = [(raw[group, a, 0, member, at], raw[group, a, 1, member, at]) for a in range(quarter)]
                for k, done in enumerate(outputs(values, near_pairs)):
                    both[group, k, member, at] = done + own[group, k, member, at]

            tiles(body)
            copy_far(group).start()
            copy_far_outer(group).start()

    length = STEPS * LANES * GAP * devices
    lanes = lax.broadcasted_iota(jnp.int32, (tall, LANES), 1)
    lines = lax.broadcasted_iota(jnp.int32, (tall, LANES), 0)
    base = plane.astype(jnp.float32) * 0.25 - 0.5

    def finish(group, gather):
        def body(member, at, first):
            row = (place * SPLIT + group % SPLIT) * depth + first
            slot = ((lines + row) * LANES + lanes) * GAP
            within = (slot + group // SPLIT).astype(jnp.float32) / length
            for kk in range(quarter):
                centred = (base + kk / devices) + within
                weight = jnp.exp(RATE * centred * centred) * length**-0.5
                total[group, kk, member, at] = gather(kk, member, at) * weight

        tiles(body)

    def edges(end):
        row = 0 if end else depth - 1
        shift = 1 if end else -1

        @pl.loop(0, quarter)
        def _(kk):
            for p in range(RADIX):
                edge[kk, p : p + 1] = total[p * SPLIT + (0 if end else SPLIT - 1), kk, :, row]

        @pl.loop(0, quarter)
        def _(kk):
            target = plane * quarter + kk - shift
            inside = jnp.logical_and(target >= 0, target < devices)

            @pl.when(jnp.logical_and(inside, target != me))
            def _():
                copy_edge(kk, end).start()

    def edges_sent(end):
        shift = 1 if end else -1

        @pl.loop(0, quarter)
        def _(kk):
            target = plane * quarter + kk - shift
            inside = jnp.logical_and(target >= 0, target < devices)

            @pl.when(jnp.logical_and(inside, target != me))
            def _():
                copy_edge(kk, end).wait_send()

    def last_stage(group):
        copy_far(group).wait_recv()

        @pl.when(is_outer)
        def _():
            copy_near(group).wait_recv()
            finish(
                group,
                lambda kk, member, at: own[group, plane * quarter + kk, member, at]
                + (arrived[group, 1, kk, member, at] + arrived[group, 0, kk, member, at]),
            )

        @pl.when(is_inner)
        def _():
            finish(
                group,
                lambda kk, member, at: both[group, plane * quarter + kk, member, at] + arrived[group, 0, kk, member, at],
            )

        @pl.when(group == groups - 1)
        def _():
            for end in range(2):
                @pl.when(place == (0 if end else quarter - 1))
                def _():
                    edges(end)

        @pl.loop(1, quarter)
        def _(step):
            copy_b(group, beside(step)).start()

        out_ref[group, place] = total[group, place]

    stages = ((0, first_stage), (1, second_stage), (3, third_stage), (5, last_stage))

    @pl.loop(0, groups + 5)
    def _(turn):
        for lag, stage in stages:
            @pl.when(jnp.logical_and(turn >= lag, turn < groups + lag))
            def _():
                stage(turn - lag)

    for end in range(2):
        sender = 0 if end else quarter - 1
        bound = devices - 1 if end else 0

        @pl.when(me == bound)
        def _():
            halo_ref[end] = jnp.zeros(halo_ref.shape[1:], jnp.float32)

        @pl.when(jnp.logical_and(me != bound, place == sender))
        def _():
            halo_ref[end] = edge[sender + (1 if end else -1)]

        @pl.when(jnp.logical_and(me != bound, place != sender))
        def _():
            copy_edge(0, end).wait_recv()

    @pl.loop(0, groups)
    def _(group):
        whole(out_ref, group, sem_sb, sem_rb).wait_recv()

    for end in range(2):
        @pl.when(place == (0 if end else quarter - 1))
        def _():
            edges_sent(end)

    @pl.loop(0, groups)
    def _(group):
        whole(send_a, group, sem_sa, sem_ra).wait_send()
        whole(total, group, sem_sb, sem_rb).wait_send()

        @pl.when(is_outer)
        def _():
            copy_raw(group).wait_send()

        @pl.when(is_inner)
        def _():
            copy_far(group).wait_send()
            copy_far_outer(group).wait_send()
            copy_near(group).wait_send()


def across(samples, inner, outer):
    devices = inner * outer
    seg = samples.shape[2]
    length = seg * devices
    me = lax.axis_index("inner") * outer + lax.axis_index("outer")
    quarter = devices // 4
    depth = STEPS // (quarter * SPLIT)
    per = 1
    x = samples.reshape(2, RADIX, STEPS, LANES)

    def phase(number, order):
        angle = number.astype(jnp.float32) * (-TAU / order)
        return jnp.cos(angle), jnp.sin(angle)

    f = lax.broadcasted_iota(jnp.int32, (STEPS, LANES), 0)
    u = jnp.stack(phase(f * (lax.broadcasted_iota(jnp.int32, (STEPS, LANES), 1) * devices + me), length // RADIX))
    p = lax.broadcasted_iota(jnp.int32, (RADIX, LANES), 0)
    v = jnp.stack(phase(p * (lax.broadcasted_iota(jnp.int32, (RADIX, LANES), 1) * devices + me), length))
    g = lax.broadcasted_iota(jnp.int32, (LANES, LANES), 0)
    order = LANES * devices
    number = g * (lax.broadcasted_iota(jnp.int32, (LANES, LANES), 1) * devices + me) % order
    cosine, sine = phase(number, order)
    last = jnp.concatenate(
        [jnp.concatenate([cosine, -sine], axis=1), jnp.concatenate([sine, cosine], axis=1)], axis=0
    )
    vmem = pl.BlockSpec(memory_space=pltpu.VMEM)
    first = (GROUPS, quarter, 2, per, depth, LANES)
    block = (GROUPS, quarter, per, depth, LANES)
    wide = (GROUPS, devices, per, depth, LANES)
    return pl.pallas_call(
        functools.partial(across_kernel, inner, outer),
        out_shape=(
            jax.ShapeDtypeStruct(block, jnp.float32),
            jax.ShapeDtypeStruct((2, RADIX, LANES), jnp.float32),
        ),
        in_specs=[pl.BlockSpec(memory_space=pltpu.HBM)] * 2 + [vmem] * 3,
        out_specs=(vmem, vmem),
        scratch_shapes=[
            pltpu.VMEM(x.shape, jnp.float32),
            pltpu.VMEM((RADIX, 4, STEPS, STEPS), jnp.bfloat16),
            pltpu.VMEM((RADIX, STEPS, 2 * LANES), jnp.float32),
            pltpu.VMEM((2, STEPS, LANES), jnp.float32),
            pltpu.VMEM(first, jnp.float32),
            pltpu.VMEM(first, jnp.float32),
            pltpu.VMEM(first, jnp.float32),
            pltpu.VMEM(wide, jnp.float32),
            pltpu.VMEM(wide, jnp.float32),
            pltpu.VMEM((GROUPS, 2, quarter, per, depth, LANES), jnp.float32),
            pltpu.VMEM(block, jnp.float32),
            pltpu.VMEM((quarter, RADIX, LANES), jnp.float32),
        ]
        + [pltpu.SemaphoreType.DMA((2,)), pltpu.SemaphoreType.DMA((RADIX,))]
        + [pltpu.SemaphoreType.DMA((GROUPS,))] * 4
        + [pltpu.SemaphoreType.DMA((GROUPS, 3)), pltpu.SemaphoreType.DMA((GROUPS, 2))]
        + [pltpu.SemaphoreType.DMA((GROUPS,))] * 2
        + [pltpu.SemaphoreType.DMA((quarter,)), pltpu.SemaphoreType.DMA((2,))],
        compiler_params=pltpu.CompilerParams(
            collective_id=0, has_side_effects=True, vmem_limit_bytes=48 * 2**20
        ),
    )(x, jnp.asarray(stage_table()), u, v, last)


def gram_kernel(inner, outer, real_ref, halo_ref, index_ref, offset_ref, weight_ref, order_ref, z_ref, gram_ref, field):
    devices = inner * outer
    groups, _, per, depth, _ = real_ref.shape

    @pl.loop(0, devices // 4)
    def _(e):
        for share in range(SPLIT):
            at = pl.ds(pl.multiple_of(8 + (e * SPLIT + share) * depth, math.gcd(8, depth)), depth)
            for p in range(GAP):
                field[p, at, :] = real_ref[p * SPLIT + share, e, 0]

    field[:, 7:8, :] = halo_ref[0][:, None, :]
    field[:, STEPS + 8 : STEPS + 9, :] = halo_ref[1][:, None, :]

    lane = lax.broadcasted_iota(jnp.int32, (8, LANES), 1)

    @pl.loop(0, STEPS // 8, unroll=2)
    def _(tile):
        row = pl.multiple_of(tile * 8, 8)
        index = index_ref[pl.ds(row, 8)]
        offset = offset_ref[pl.ds(row, 8)]
        samples = {}
        for p in range(GAP):
            now = field[p, pl.ds(row + 8, 8)]
            before = field[p, pl.ds(row + 7, 8)]
            after = field[p, pl.ds(row + 9, 8)]
            for slot in (-2, -1, 0, 1, 2):
                place = GAP * slot + p
                if place < 1 - HALF or place > HALF + GAP - 1:
                    continue
                if slot < 0:
                    value = pltpu.roll(jnp.where(lane >= LANES + slot, before, now), -slot, 1)
                elif slot > 0:
                    value = pltpu.roll(jnp.where(lane < slot, after, now), LANES - slot, 1)
                else:
                    value = now
                samples[place] = value
        window = [samples[place] for place in range(1 - HALF, HALF + GAP)]
        for bit in (4, 2, 1):
            chosen = (index & bit) != 0
            window = [jnp.where(chosen, b, a) for a, b in zip(window[:-bit], window[bit:])]
        total = jnp.zeros((8, LANES), jnp.float32)
        for tap in range(2 * HALF):
            total += window[tap] * jnp.take_along_axis(weight_ref[tap], offset, axis=1)
        gram_ref[pl.ds(row, 8)] = total

    width = 2 * LANES
    share = width // GAP
    run = lax.broadcasted_iota(jnp.int32, (STEPS, LANES), 1) // share
    for column in range(LANES // share):
        packed = []
        for first in range(0, GAP, LANES // share):
            piece = None
            for place in range(LANES // share):
                value = field[first + place, 8 : STEPS + 8, :]
                turn = (place - column) * share % LANES
                value = pltpu.roll(value, turn, 1) if turn else value
                piece = value if piece is None else jnp.where(run == place, value, piece)
            packed.append(piece)
        rest = jnp.concatenate(packed, axis=1)
        block = None
        for _ in range(3):
            piece = rest.astype(jnp.bfloat16)
            rest = rest - piece.astype(jnp.float32)
            product = jnp.dot(piece, order_ref[...], preferred_element_type=jnp.float32)
            block = product if block is None else block + product
        for side in range(2):
            z_ref[pl.ds(2 * column + side, STEPS, stride=GAP), :] = block[:, side * LANES : (side + 1) * LANES]


def local(inner, outer, samples, gram_index, gram_offset):
    real, halo = across(samples, inner, outer)
    rows = (STEPS, LANES)
    z, gram = pl.pallas_call(
        functools.partial(gram_kernel, inner, outer),
        out_shape=(
            jax.ShapeDtypeStruct((STEPS * GAP, LANES), jnp.float32),
            jax.ShapeDtypeStruct(rows, jnp.float32),
        ),
        in_specs=[pl.BlockSpec(memory_space=pltpu.VMEM)] * 6,
        out_specs=(pl.BlockSpec(memory_space=pltpu.VMEM),) * 2,
        scratch_shapes=[pltpu.VMEM((GAP, STEPS + 16, LANES), jnp.float32)],
        compiler_params=pltpu.CompilerParams(vmem_limit_bytes=48 * 2**20),
    )(
        real, halo, gram_index.reshape(rows), gram_offset.reshape(rows),
        jnp.asarray(weight_table()), jnp.asarray(order_table()),
    )
    return z.reshape(-1), gram.reshape(-1)


def solution(mesh):
    return jax.shard_map(
        functools.partial(local, mesh.shape["inner"], mesh.shape["outer"]),
        mesh=mesh,
        in_specs=(P(None, ("inner", "outer"), None), P(("inner", "outer")), P(("inner", "outer"))),
        out_specs=(P(("inner", "outer")), P(("inner", "outer"))),
        check_vma=False,
    )
```

```python
import functools
import math

import jax
import jax.numpy as jnp
import numpy as np
from jax import lax
from jax.experimental import pallas as pl
from jax.experimental.pallas import tpu as pltpu
from jax.sharding import PartitionSpec as P

GAP = 8
HALF = 16
UPS = 32
LANES = 128
RADIX = 8
STEPS = 256
SPLIT = 4
GROUPS = RADIX * SPLIT
TAU = 2.0 * math.pi
RATE = 4.0
MESH = pl.DeviceIdType.MESH
NT = (((1,), (1,)), ((), ()))


def halves(x):
    high = x.astype(jnp.bfloat16)
    low = (x - high.astype(jnp.float32)).astype(jnp.bfloat16)
    return high, low


def np_halves(x):
    x = x.astype(np.float32)
    high = x.astype(jnp.bfloat16)
    low = (x - high.astype(np.float32)).astype(jnp.bfloat16)
    return high, low


def stage_table():
    p = np.arange(RADIX)[:, None, None]
    f = np.arange(STEPS)[None, :, None]
    t = np.arange(STEPS)[None, None, :]
    order = RADIX * STEPS
    angle = (t * (RADIX * f + p) % order) * (-TAU / order)
    return np.stack([*np_halves(np.cos(angle)), *np_halves(np.sin(angle))], axis=1)


def order_table():
    size = 2 * LANES
    p, l = np.divmod(np.arange(size), size // GAP)
    table = np.zeros((size, size), np.float32)
    table[np.arange(size), GAP * l + p] = 1.0
    return table.astype(jnp.bfloat16)


def weight_table():
    tap = np.arange(1 - HALF, HALF + 1)[:, None]
    distance = np.arange(LANES)[None, :] % UPS / UPS - tap
    spread = HALF / 2.0
    table = np.sinc(distance) * np.exp(-distance * distance / (2.0 * spread * spread))
    return np.broadcast_to(table.astype(np.float32)[:, None, :], (2 * HALF, 8, LANES)).copy()


def radix_8(parts):
    def add(u, v):
        return u[0] + v[0], u[1] + v[1]

    def sub(u, v):
        return u[0] - v[0], u[1] - v[1]

    def turn(u):
        return u[1], -u[0]

    def four(a, b, c, d):
        s, t, u, v = add(a, c), sub(a, c), add(b, d), turn(sub(b, d))
        return add(s, u), add(t, v), sub(s, u), sub(t, v)

    even = four(parts[0], parts[2], parts[4], parts[6])
    odd = four(parts[1], parts[3], parts[5], parts[7])
    r = math.sqrt(0.5)
    odd = (
        odd[0],
        ((odd[1][0] + odd[1][1]) * r, (odd[1][1] - odd[1][0]) * r),
        turn(odd[2]),
        ((odd[3][1] - odd[3][0]) * r, -(odd[3][0] + odd[3][1]) * r),
    )
    return [add(e, o) for e, o in zip(even, odd)] + [sub(e, o) for e, o in zip(even, odd)]


def transform(values):
    size = len(values)
    if size == 1:
        return values
    even, odd = transform(values[0::2]), transform(values[1::2])
    first, second = [], []
    for k in range(size // 2):
        (er, ei), (br, bi) = even[k], odd[k]
        if k == 0:
            tr, ti = br, bi
        elif 4 * k == size:
            tr, ti = bi, -br
        else:
            c, s = math.cos(TAU * k / size), -math.sin(TAU * k / size)
            tr, ti = br * c - bi * s, br * s + bi * c
        first.append((er + tr, ei + ti))
        second.append((er - tr, ei - ti))
    return first + second


def real_transform(values):
    size = len(values)
    even, odd = transform(values[0::2]), transform(values[1::2])
    first, second = [], []
    for k in range(size // 2):
        c, s = math.cos(TAU * k / size), -math.sin(TAU * k / size)
        t = odd[k][0] if k == 0 else odd[k][1] if 4 * k == size else odd[k][0] * c - odd[k][1] * s
        first.append(even[k][0] + t)
        second.append(even[k][0] - t)
    return first + second


def across_kernel(
    inner, outer, x_hbm, stage_hbm, u_ref, v_ref, last_ref, out_ref, halo_ref,
    x_ref, stage_ref, parts, rows, send_a, recv_a, raw, own, both, arrived, total, edge,
    sem_x, sem_t, sem_sa, sem_ra, sem_sw, sem_rw, sem_sp, sem_rp, sem_sb, sem_rb, sem_se, sem_re,
):
    devices = inner * outer
    me = lax.axis_index("inner") * outer + lax.axis_index("outer")
    groups, quarter, _, per, depth, _ = send_a.shape
    plane = me // quarter
    place = me % quarter
    near_plane = plane + 1 - 2 * (plane % 2)
    far_plane = 3 - plane
    far_outer = far_plane + 1 - 2 * (far_plane % 2)
    is_outer = jnp.logical_or(plane == 0, plane == 3)
    is_inner = jnp.logical_not(is_outer)

    def where(device):
        return (device // outer, device % outer)

    def beside(step):
        return plane * quarter + (place + step) % quarter

    def load_x(part):
        return pltpu.make_async_copy(x_hbm.at[part], x_ref.at[part], sem_x.at[part])

    def load_table(p):
        return pltpu.make_async_copy(stage_hbm.at[p], stage_ref.at[p], sem_t.at[p])

    for part in range(2):
        load_x(part).start()

    @pl.loop(0, RADIX)
    def _(p):
        load_table(p).start()

    barrier = pltpu.get_barrier_semaphore()

    @pl.loop(1, devices)
    def _(step):
        pl.semaphore_signal(barrier, inc=1, device_id=where((me + step) % devices), device_id_type=MESH)

    for part in range(2):
        load_x(part).wait()

    @pl.loop(0, STEPS // 32)
    def _(tile):
        at = pl.ds(pl.multiple_of(tile * 32, 32), 32)
        done = radix_8([(x_ref[0, q, at], x_ref[1, q, at]) for q in range(RADIX)])
        for p in range(RADIX):
            parts[p, at, :LANES] = done[p][0]
            parts[p, at, LANES:] = done[p][1]

    def dot(a, b):
        return jnp.dot(a, b, preferred_element_type=jnp.float32)

    def dot_nt(a, b):
        return lax.dot_general(a, b, NT, preferred_element_type=jnp.float32)

    def send(source, target_ref, sent, here, device):
        return pltpu.make_async_remote_copy(
            src_ref=source, dst_ref=target_ref, send_sem=sent, recv_sem=here,
            device_id=where(device), device_id_type=MESH,
        )

    def copy_a(group, target):
        return send(
            send_a.at[group, target % quarter], recv_a.at[group, place], sem_sa.at[group], sem_ra.at[group], target
        )

    def copy_b(group, target):
        return send(
            total.at[group, target % quarter], out_ref.at[group, place], sem_sb.at[group], sem_rb.at[group], target
        )

    def copy_raw(group):
        return send(
            recv_a.at[group], raw.at[group], sem_sw.at[group], sem_rw.at[group], near_plane * quarter + place
        )

    def copy_part(source, group, slot, number, to_plane):
        return send(
            source.at[group, pl.ds(to_plane * quarter, quarter)], arrived.at[group, slot],
            sem_sp.at[group, number], sem_rp.at[group, slot], to_plane * quarter + place,
        )

    def copy_far(group):
        return copy_part(both, group, 0, 0, far_plane)

    def copy_far_outer(group):
        return copy_part(both, group, 0, 1, far_outer)

    def copy_near(group):
        return copy_part(own, group, 1, 2, near_plane)

    def whole(ref, group, sem_sent, sem_here):
        part = ref.at[group, pl.ds(0, quarter - 1)]
        return send(part, part, sem_sent.at[group], sem_here.at[group], beside(1))

    def copy_edge(kk, end):
        target = (plane * quarter + kk - (1 if end else -1) + devices) % devices
        return send(edge.at[kk], halo_ref.at[end], sem_se.at[kk], sem_re.at[end], target)

    last_high, last_low = halves(last_ref[...])

    def spectrum(p):
        load_table(p).wait()
        high, low = halves(parts[p])
        cos_high, cos_low, sin_high, sin_low = (stage_ref[p, i] for i in range(4))
        by_cos = dot(cos_high, high) + dot(cos_high, low) + dot(cos_low, high)
        by_sin = dot(sin_high, high) + dot(sin_high, low) + dot(sin_low, high)
        real = by_cos[:, :LANES] - by_sin[:, LANES:]
        imag = by_cos[:, LANES:] + by_sin[:, :LANES]
        vr, vi = v_ref[0, pl.ds(p, 1)], v_ref[1, pl.ds(p, 1)]
        ur, ui = u_ref[0], u_ref[1]
        tr, ti = ur * vr - ui * vi, ur * vi + ui * vr
        both = jnp.concatenate([real * tr - imag * ti, real * ti + imag * tr], axis=1)
        high, low = halves(both)
        z = dot_nt(last_high, high) + dot_nt(last_high, low) + dot_nt(last_low, high)
        for part in range(2):
            block = z[part * LANES : (part + 1) * LANES]
            for lane_half in range(2):
                rows[part, pl.ds(lane_half, LANES, stride=2), :] = block[:, lane_half * LANES : (lane_half + 1) * LANES]
            value = rows[part].reshape(quarter, SPLIT, depth, LANES)
            for share in range(SPLIT):
                send_a[p * SPLIT + share, :, part, 0] = value[:, share]

    def spectra(group):
        @pl.when(group % SPLIT == 0)
        def _():
            spectrum(group // SPLIT)

        recv_a[group, place] = send_a[group, place]

    def factors(which):
        pairs = []
        for v in range(4):
            turns = (which * v) % 4
            real = jnp.where(turns == 0, 1.0, jnp.where(turns == 2, -1.0, 0.0))
            imag = jnp.where(turns == 1, -1.0, jnp.where(turns == 3, 1.0, 0.0))
            pairs.append((real, imag))
        return pairs

    def outputs(values, pairs):
        result = [None] * devices
        for v in range(4):
            turned = []
            for a, (vr, vi) in enumerate(values):
                c, s = math.cos(TAU * a * v / devices), -math.sin(TAU * a * v / devices)
                turned.append((vr, vi) if a * v == 0 else (vr * c - vi * s, vr * s + vi * c))
            for u, (real, imag) in enumerate(transform(turned)):
                result[4 * u + v] = real if v == 0 else real * pairs[v][0] - imag * pairs[v][1]
        return result

    tall = min(8, depth)

    def tiles(body):
        @pl.loop(0, per)
        def _(member):
            @pl.loop(0, depth // tall)
            def _(tile):
                body(member, pl.ds(pl.multiple_of(tile * tall, tall), tall), tile * tall)

    own_pairs, near_pairs = factors(plane), factors(near_plane)

    def first_stage(group):
        spectra(group)

        @pl.when(group == 0)
        def _():
            pl.semaphore_wait(barrier, devices - 1)

        @pl.loop(1, quarter)
        def _(step):
            copy_a(group, beside(step)).start()

    def second_stage(group):
        whole(recv_a, group, sem_sa, sem_ra).wait_recv()

        @pl.when(is_outer)
        def _():
            copy_raw(group).start()

        def body(member, at, first):
            values = [(recv_a[group, a, 0, member, at], recv_a[group, a, 1, member, at]) for a in range(quarter)]
            for k, done in enumerate(outputs(values, own_pairs)):
                own[group, k, member, at] = done

        tiles(body)

        @pl.when(is_inner)
        def _():
            copy_near(group).start()

    def third_stage(group):
        @pl.when(is_inner)
        def _():
            copy_raw(group).wait_recv()

            def body(member, at, first):
                values = [(raw[group, a, 0, member, at], raw[group, a, 1, member, at]) for a in range(quarter)]
                for k, done in enumerate(outputs(values, near_pairs)):
                    both[group, k, member, at] = done + own[group, k, member, at]

            tiles(body)
            copy_far_outer(group).start()
            copy_far(group).start()

    length = STEPS * LANES * GAP * devices
    lanes = lax.broadcasted_iota(jnp.int32, (tall, LANES), 1)
    lines = lax.broadcasted_iota(jnp.int32, (tall, LANES), 0)
    base = plane.astype(jnp.float32) * 0.25 - 0.5

    def finish(group, gather):
        def body(member, at, first):
            row = (place * SPLIT + group % SPLIT) * depth + first
            slot = ((lines + row) * LANES + lanes) * GAP
            within = (slot + group // SPLIT).astype(jnp.float32) / length
            for kk in range(quarter):
                centred = (base + kk / devices) + within
                weight = jnp.exp(RATE * centred * centred) * length**-0.5
                total[group, kk, member, at] = gather(kk, member, at) * weight

        tiles(body)

    def edges(end):
        row = 0 if end else depth - 1
        shift = 1 if end else -1

        @pl.loop(0, quarter)
        def _(kk):
            for p in range(RADIX):
                edge[kk, p : p + 1] = total[p * SPLIT + (0 if end else SPLIT - 1), kk, :, row]

        @pl.loop(0, quarter)
        def _(kk):
            target = plane * quarter + kk - shift
            inside = jnp.logical_and(target >= 0, target < devices)

            @pl.when(jnp.logical_and(inside, target != me))
            def _():
                copy_edge(kk, end).start()

    def edges_sent(end):
        shift = 1 if end else -1

        @pl.loop(0, quarter)
        def _(kk):
            target = plane * quarter + kk - shift
            inside = jnp.logical_and(target >= 0, target < devices)

            @pl.when(jnp.logical_and(inside, target != me))
            def _():
                copy_edge(kk, end).wait_send()

    def last_stage(group):
        copy_far(group).wait_recv()

        @pl.when(is_outer)
        def _():
            copy_near(group).wait_recv()
            finish(
                group,
                lambda kk, member, at: own[group, plane * quarter + kk, member, at]
                + (arrived[group, 1, kk, member, at] + arrived[group, 0, kk, member, at]),
            )

        @pl.when(is_inner)
        def _():
            finish(
                group,
                lambda kk, member, at: both[group, plane * quarter + kk, member, at] + arrived[group, 0, kk, member, at],
            )

        @pl.when(group == groups - 1)
        def _():
            for end in range(2):
                @pl.when(place == (0 if end else quarter - 1))
                def _():
                    edges(end)

        @pl.loop(1, quarter)
        def _(step):
            copy_b(group, beside(step)).start()

        out_ref[group, place] = total[group, place]

    stages = ((0, first_stage), (2, second_stage), (5, third_stage), (9, last_stage))

    @pl.loop(0, groups + 9)
    def _(turn):
        for lag, stage in stages:
            @pl.when(jnp.logical_and(turn >= lag, turn < groups + lag))
            def _():
                stage(turn - lag)

    for end in range(2):
        sender = 0 if end else quarter - 1
        bound = devices - 1 if end else 0

        @pl.when(me == bound)
        def _():
            halo_ref[end] = jnp.zeros(halo_ref.shape[1:], jnp.float32)

        @pl.when(jnp.logical_and(me != bound, place == sender))
        def _():
            halo_ref[end] = edge[sender + (1 if end else -1)]

        @pl.when(jnp.logical_and(me != bound, place != sender))
        def _():
            copy_edge(0, end).wait_recv()

    @pl.loop(0, groups)
    def _(group):
        whole(out_ref, group, sem_sb, sem_rb).wait_recv()

    for end in range(2):
        @pl.when(place == (0 if end else quarter - 1))
        def _():
            edges_sent(end)

    @pl.loop(0, groups)
    def _(group):
        whole(send_a, group, sem_sa, sem_ra).wait_send()
        whole(total, group, sem_sb, sem_rb).wait_send()

        @pl.when(is_outer)
        def _():
            copy_raw(group).wait_send()

        @pl.when(is_inner)
        def _():
            copy_far(group).wait_send()
            copy_far_outer(group).wait_send()
            copy_near(group).wait_send()


def across(samples, inner, outer):
    devices = inner * outer
    seg = samples.shape[2]
    length = seg * devices
    me = lax.axis_index("inner") * outer + lax.axis_index("outer")
    quarter = devices // 4
    depth = STEPS // (quarter * SPLIT)
    per = 1
    x = samples.reshape(2, RADIX, STEPS, LANES)

    def phase(number, order):
        angle = number.astype(jnp.float32) * (-TAU / order)
        return jnp.cos(angle), jnp.sin(angle)

    f = lax.broadcasted_iota(jnp.int32, (STEPS, LANES), 0)
    u = jnp.stack(phase(f * (lax.broadcasted_iota(jnp.int32, (STEPS, LANES), 1) * devices + me), length // RADIX))
    p = lax.broadcasted_iota(jnp.int32, (RADIX, LANES), 0)
    v = jnp.stack(phase(p * (lax.broadcasted_iota(jnp.int32, (RADIX, LANES), 1) * devices + me), length))
    g = lax.broadcasted_iota(jnp.int32, (LANES, LANES), 0)
    order = LANES * devices
    number = g * (lax.broadcasted_iota(jnp.int32, (LANES, LANES), 1) * devices + me) % order
    cosine, sine = phase(number, order)
    last = jnp.concatenate(
        [jnp.concatenate([cosine, -sine], axis=1), jnp.concatenate([sine, cosine], axis=1)], axis=0
    )
    vmem = pl.BlockSpec(memory_space=pltpu.VMEM)
    first = (GROUPS, quarter, 2, per, depth, LANES)
    block = (GROUPS, quarter, per, depth, LANES)
    wide = (GROUPS, devices, per, depth, LANES)
    return pl.pallas_call(
        functools.partial(across_kernel, inner, outer),
        out_shape=(
            jax.ShapeDtypeStruct(block, jnp.float32),
            jax.ShapeDtypeStruct((2, RADIX, LANES), jnp.float32),
        ),
        in_specs=[pl.BlockSpec(memory_space=pltpu.HBM)] * 2 + [vmem] * 3,
        out_specs=(vmem, vmem),
        scratch_shapes=[
            pltpu.VMEM(x.shape, jnp.float32),
            pltpu.VMEM((RADIX, 4, STEPS, STEPS), jnp.bfloat16),
            pltpu.VMEM((RADIX, STEPS, 2 * LANES), jnp.float32),
            pltpu.VMEM((2, STEPS, LANES), jnp.float32),
            pltpu.VMEM(first, jnp.float32),
            pltpu.VMEM(first, jnp.float32),
            pltpu.VMEM(first, jnp.float32),
            pltpu.VMEM(wide, jnp.float32),
            pltpu.VMEM(wide, jnp.float32),
            pltpu.VMEM((GROUPS, 2, quarter, per, depth, LANES), jnp.float32),
            pltpu.VMEM(block, jnp.float32),
            pltpu.VMEM((quarter, RADIX, LANES), jnp.float32),
        ]
        + [pltpu.SemaphoreType.DMA((2,)), pltpu.SemaphoreType.DMA((RADIX,))]
        + [pltpu.SemaphoreType.DMA((GROUPS,))] * 4
        + [pltpu.SemaphoreType.DMA((GROUPS, 3)), pltpu.SemaphoreType.DMA((GROUPS, 2))]
        + [pltpu.SemaphoreType.DMA((GROUPS,))] * 2
        + [pltpu.SemaphoreType.DMA((quarter,)), pltpu.SemaphoreType.DMA((2,))],
        compiler_params=pltpu.CompilerParams(
            collective_id=0, has_side_effects=True, vmem_limit_bytes=48 * 2**20
        ),
    )(x, jnp.asarray(stage_table()), u, v, last)


def gram_kernel(inner, outer, real_ref, halo_ref, index_ref, offset_ref, weight_ref, order_ref, z_ref, gram_ref, field):
    devices = inner * outer
    groups, _, per, depth, _ = real_ref.shape

    @pl.loop(0, devices // 4)
    def _(e):
        for share in range(SPLIT):
            at = pl.ds(pl.multiple_of(8 + (e * SPLIT + share) * depth, math.gcd(8, depth)), depth)
            for p in range(GAP):
                field[p, at, :] = real_ref[p * SPLIT + share, e, 0]

    field[:, 7:8, :] = halo_ref[0][:, None, :]
    field[:, STEPS + 8 : STEPS + 9, :] = halo_ref[1][:, None, :]

    lane = lax.broadcasted_iota(jnp.int32, (8, LANES), 1)

    @pl.loop(0, STEPS // 8, unroll=2)
    def _(tile):
        row = pl.multiple_of(tile * 8, 8)
        index = index_ref[pl.ds(row, 8)]
        offset = offset_ref[pl.ds(row, 8)]
        samples = {}
        for p in range(GAP):
            now = field[p, pl.ds(row + 8, 8)]
            before = field[p, pl.ds(row + 7, 8)]
            after = field[p, pl.ds(row + 9, 8)]
            for slot in (-2, -1, 0, 1, 2):
                place = GAP * slot + p
                if place < 1 - HALF or place > HALF + GAP - 1:
                    continue
                if slot < 0:
                    value = pltpu.roll(jnp.where(lane >= LANES + slot, before, now), -slot, 1)
                elif slot > 0:
                    value = pltpu.roll(jnp.where(lane < slot, after, now), LANES - slot, 1)
                else:
                    value = now
                samples[place] = value
        window = [samples[place] for place in range(1 - HALF, HALF + GAP)]
        for bit in (4, 2, 1):
            chosen = (index & bit) != 0
            window = [jnp.where(chosen, b, a) for a, b in zip(window[:-bit], window[bit:])]
        total = jnp.zeros((8, LANES), jnp.float32)
        for tap in range(2 * HALF):
            total += window[tap] * jnp.take_along_axis(weight_ref[tap], offset, axis=1)
        gram_ref[pl.ds(row, 8)] = total

    width = 2 * LANES
    share = width // GAP
    run = lax.broadcasted_iota(jnp.int32, (STEPS, LANES), 1) // share
    for column in range(LANES // share):
        packed = []
        for first in range(0, GAP, LANES // share):
            piece = None
            for place in range(LANES // share):
                value = field[first + place, 8 : STEPS + 8, :]
                turn = (place - column) * share % LANES
                value = pltpu.roll(value, turn, 1) if turn else value
                piece = value if piece is None else jnp.where(run == place, value, piece)
            packed.append(piece)
        rest = jnp.concatenate(packed, axis=1)
        block = None
        for _ in range(3):
            piece = rest.astype(jnp.bfloat16)
            rest = rest - piece.astype(jnp.float32)
            product = jnp.dot(piece, order_ref[...], preferred_element_type=jnp.float32)
            block = product if block is None else block + product
        for side in range(2):
            z_ref[pl.ds(2 * column + side, STEPS, stride=GAP), :] = block[:, side * LANES : (side + 1) * LANES]


def local(inner, outer, samples, gram_index, gram_offset):
    real, halo = across(samples, inner, outer)
    rows = (STEPS, LANES)
    z, gram = pl.pallas_call(
        functools.partial(gram_kernel, inner, outer),
        out_shape=(
            jax.ShapeDtypeStruct((STEPS * GAP, LANES), jnp.float32),
            jax.ShapeDtypeStruct(rows, jnp.float32),
        ),
        in_specs=[pl.BlockSpec(memory_space=pltpu.VMEM)] * 6,
        out_specs=(pl.BlockSpec(memory_space=pltpu.VMEM),) * 2,
        scratch_shapes=[pltpu.VMEM((GAP, STEPS + 16, LANES), jnp.float32)],
        compiler_params=pltpu.CompilerParams(vmem_limit_bytes=48 * 2**20),
    )(
        real, halo, gram_index.reshape(rows), gram_offset.reshape(rows),
        jnp.asarray(weight_table()), jnp.asarray(order_table()),
    )
    return z.reshape(-1), gram.reshape(-1)


def solution(mesh):
    return jax.shard_map(
        functools.partial(local, mesh.shape["inner"], mesh.shape["outer"]),
        mesh=mesh,
        in_specs=(P(None, ("inner", "outer"), None), P(("inner", "outer")), P(("inner", "outer"))),
        out_specs=(P(("inner", "outer")), P(("inner", "outer"))),
        check_vma=False,
    )
```

```python
import functools
import math

import jax
import jax.numpy as jnp
import numpy as np
from jax import lax
from jax.experimental import pallas as pl
from jax.experimental.pallas import tpu as pltpu
from jax.sharding import PartitionSpec as P

GAP = 8
HALF = 16
UPS = 32
LANES = 128
RADIX = 8
STEPS = 256
SPLIT = 2
GROUPS = RADIX * SPLIT
TAU = 2.0 * math.pi
RATE = 4.0
MESH = pl.DeviceIdType.MESH
NT = (((1,), (1,)), ((), ()))


def halves(x):
    high = x.astype(jnp.bfloat16)
    low = (x - high.astype(jnp.float32)).astype(jnp.bfloat16)
    return high, low


def np_halves(x):
    x = x.astype(np.float32)
    high = x.astype(jnp.bfloat16)
    low = (x - high.astype(np.float32)).astype(jnp.bfloat16)
    return high, low


def stage_table():
    p = np.arange(RADIX)[:, None, None]
    f = np.arange(STEPS)[None, :, None]
    t = np.arange(STEPS)[None, None, :]
    order = RADIX * STEPS
    angle = (t * (RADIX * f + p) % order) * (-TAU / order)
    return np.stack([*np_halves(np.cos(angle)), *np_halves(np.sin(angle))], axis=1)


def order_table():
    size = 2 * LANES
    p, l = np.divmod(np.arange(size), size // GAP)
    table = np.zeros((size, size), np.float32)
    table[np.arange(size), GAP * l + p] = 1.0
    return table.astype(jnp.bfloat16)


def weight_table():
    tap = np.arange(1 - HALF, HALF + 1)[:, None]
    distance = np.arange(LANES)[None, :] % UPS / UPS - tap
    spread = HALF / 2.0
    table = np.sinc(distance) * np.exp(-distance * distance / (2.0 * spread * spread))
    return np.broadcast_to(table.astype(np.float32)[:, None, :], (2 * HALF, 8, LANES)).copy()


def radix_8(parts):
    def add(u, v):
        return u[0] + v[0], u[1] + v[1]

    def sub(u, v):
        return u[0] - v[0], u[1] - v[1]

    def turn(u):
        return u[1], -u[0]

    def four(a, b, c, d):
        s, t, u, v = add(a, c), sub(a, c), add(b, d), turn(sub(b, d))
        return add(s, u), add(t, v), sub(s, u), sub(t, v)

    even = four(parts[0], parts[2], parts[4], parts[6])
    odd = four(parts[1], parts[3], parts[5], parts[7])
    r = math.sqrt(0.5)
    odd = (
        odd[0],
        ((odd[1][0] + odd[1][1]) * r, (odd[1][1] - odd[1][0]) * r),
        turn(odd[2]),
        ((odd[3][1] - odd[3][0]) * r, -(odd[3][0] + odd[3][1]) * r),
    )
    return [add(e, o) for e, o in zip(even, odd)] + [sub(e, o) for e, o in zip(even, odd)]


def transform(values):
    size = len(values)
    if size == 1:
        return values
    even, odd = transform(values[0::2]), transform(values[1::2])
    first, second = [], []
    for k in range(size // 2):
        (er, ei), (br, bi) = even[k], odd[k]
        if k == 0:
            tr, ti = br, bi
        elif 4 * k == size:
            tr, ti = bi, -br
        else:
            c, s = math.cos(TAU * k / size), -math.sin(TAU * k / size)
            tr, ti = br * c - bi * s, br * s + bi * c
        first.append((er + tr, ei + ti))
        second.append((er - tr, ei - ti))
    return first + second


def real_transform(values):
    size = len(values)
    even, odd = transform(values[0::2]), transform(values[1::2])
    first, second = [], []
    for k in range(size // 2):
        c, s = math.cos(TAU * k / size), -math.sin(TAU * k / size)
        t = odd[k][0] if k == 0 else odd[k][1] if 4 * k == size else odd[k][0] * c - odd[k][1] * s
        first.append(even[k][0] + t)
        second.append(even[k][0] - t)
    return first + second


def across_kernel(
    inner, outer, x_hbm, stage_hbm, u_ref, v_ref, last_ref, out_ref, halo_ref,
    x_ref, stage_ref, parts, rows, send_a, recv_a, raw, own, both, arrived, total, edge,
    sem_x, sem_t, sem_sa, sem_ra, sem_sw, sem_rw, sem_sp, sem_rp, sem_sb, sem_rb, sem_se, sem_re,
):
    devices = inner * outer
    me = lax.axis_index("inner") * outer + lax.axis_index("outer")
    groups, quarter, _, per, depth, _ = send_a.shape
    plane = me // quarter
    place = me % quarter
    near_plane = plane + 1 - 2 * (plane % 2)
    far_plane = 3 - plane
    far_outer = far_plane + 1 - 2 * (far_plane % 2)
    is_outer = jnp.logical_or(plane == 0, plane == 3)
    is_inner = jnp.logical_not(is_outer)

    def where(device):
        return (device // outer, device % outer)

    def beside(step):
        return plane * quarter + (place + step) % quarter

    def load_x(part):
        return pltpu.make_async_copy(x_hbm.at[part], x_ref.at[part], sem_x.at[part])

    def load_table(p):
        return pltpu.make_async_copy(stage_hbm.at[p], stage_ref.at[p], sem_t.at[p])

    for part in range(2):
        load_x(part).start()

    @pl.loop(0, RADIX)
    def _(p):
        load_table(p).start()

    barrier = pltpu.get_barrier_semaphore()

    @pl.loop(1, devices)
    def _(step):
        pl.semaphore_signal(barrier, inc=1, device_id=where((me + step) % devices), device_id_type=MESH)

    for part in range(2):
        load_x(part).wait()

    @pl.loop(0, STEPS // 32)
    def _(tile):
        at = pl.ds(pl.multiple_of(tile * 32, 32), 32)
        done = radix_8([(x_ref[0, q, at], x_ref[1, q, at]) for q in range(RADIX)])
        for p in range(RADIX):
            parts[p, at, :LANES] = done[p][0]
            parts[p, at, LANES:] = done[p][1]

    def dot(a, b):
        return jnp.dot(a, b, preferred_element_type=jnp.float32)

    def dot_nt(a, b):
        return lax.dot_general(a, b, NT, preferred_element_type=jnp.float32)

    def send(source, target_ref, sent, here, device):
        return pltpu.make_async_remote_copy(
            src_ref=source, dst_ref=target_ref, send_sem=sent, recv_sem=here,
            device_id=where(device), device_id_type=MESH,
        )

    def copy_a(group, target):
        return send(
            send_a.at[group, target % quarter], recv_a.at[group, place], sem_sa.at[group], sem_ra.at[group], target
        )

    def copy_b(group, target):
        return send(
            total.at[group, target % quarter], out_ref.at[group, place], sem_sb.at[group], sem_rb.at[group], target
        )

    def copy_raw(group):
        return send(
            recv_a.at[group], raw.at[group], sem_sw.at[group], sem_rw.at[group], near_plane * quarter + place
        )

    def copy_part(source, group, slot, number, to_plane):
        return send(
            source.at[group, pl.ds(to_plane * quarter, quarter)], arrived.at[group, slot],
            sem_sp.at[group, number], sem_rp.at[group, slot], to_plane * quarter + place,
        )

    def copy_far(group):
        return copy_part(both, group, 0, 0, far_plane)

    def copy_far_outer(group):
        return copy_part(both, group, 0, 1, far_outer)

    def copy_near(group):
        return copy_part(own, group, 1, 2, near_plane)

    def whole(ref, group, sem_sent, sem_here):
        part = ref.at[group, pl.ds(0, quarter - 1)]
        return send(part, part, sem_sent.at[group], sem_here.at[group], beside(1))

    def copy_edge(kk, end):
        target = (plane * quarter + kk - (1 if end else -1) + devices) % devices
        return send(edge.at[kk], halo_ref.at[end], sem_se.at[kk], sem_re.at[end], target)

    last_high, last_low = halves(last_ref[...])

    def spectrum(p):
        load_table(p).wait()
        high, low = halves(parts[p])
        cos_high, cos_low, sin_high, sin_low = (stage_ref[p, i] for i in range(4))
        by_cos = dot(cos_high, high) + dot(cos_high, low) + dot(cos_low, high)
        by_sin = dot(sin_high, high) + dot(sin_high, low) + dot(sin_low, high)
        real = by_cos[:, :LANES] - by_sin[:, LANES:]
        imag = by_cos[:, LANES:] + by_sin[:, :LANES]
        vr, vi = v_ref[0, pl.ds(p, 1)], v_ref[1, pl.ds(p, 1)]
        ur, ui = u_ref[0], u_ref[1]
        tr, ti = ur * vr - ui * vi, ur * vi + ui * vr
        both = jnp.concatenate([real * tr - imag * ti, real * ti + imag * tr], axis=1)
        high, low = halves(both)
        z = dot_nt(last_high, high) + dot_nt(last_high, low) + dot_nt(last_low, high)
        for part in range(2):
            block = z[part * LANES : (part + 1) * LANES]
            for lane_half in range(2):
                rows[part, pl.ds(lane_half, LANES, stride=2), :] = block[:, lane_half * LANES : (lane_half + 1) * LANES]
            value = rows[part].reshape(quarter, SPLIT, depth, LANES)
            for share in range(SPLIT):
                send_a[p * SPLIT + share, :, part, 0] = value[:, share]

    def spectra(group):
        @pl.when(group % SPLIT == 0)
        def _():
            spectrum(group // SPLIT)

        recv_a[group, place] = send_a[group, place]

    def factors(which):
        pairs = []
        for v in range(4):
            turns = (which * v) % 4
            real = jnp.where(turns == 0, 1.0, jnp.where(turns == 2, -1.0, 0.0))
            imag = jnp.where(turns == 1, -1.0, jnp.where(turns == 3, 1.0, 0.0))
            pairs.append((real, imag))
        return pairs

    def outputs(values, pairs):
        result = [None] * devices
        for v in range(4):
            turned = []
            for a, (vr, vi) in enumerate(values):
                c, s = math.cos(TAU * a * v / devices), -math.sin(TAU * a * v / devices)
                turned.append((vr, vi) if a * v == 0 else (vr * c - vi * s, vr * s + vi * c))
            for u, (real, imag) in enumerate(transform(turned)):
                result[4 * u + v] = real if v == 0 else real * pairs[v][0] - imag * pairs[v][1]
        return result

    tall = min(8, depth)

    def tiles(body):
        @pl.loop(0, per)
        def _(member):
            @pl.loop(0, depth // tall)
            def _(tile):
                body(member, pl.ds(pl.multiple_of(tile * tall, tall), tall), tile * tall)

    own_pairs, near_pairs = factors(plane), factors(near_plane)

    def first_stage(group):
        spectra(group)

        @pl.when(group == 0)
        def _():
            pl.semaphore_wait(barrier, devices - 1)

        @pl.loop(1, quarter)
        def _(step):
            copy_a(group, beside(step)).start()

    def second_stage(group):
        whole(recv_a, group, sem_sa, sem_ra).wait_recv()

        @pl.when(is_outer)
        def _():
            copy_raw(group).start()

        def body(member, at, first):
            values = [(recv_a[group, a, 0, member, at], recv_a[group, a, 1, member, at]) for a in range(quarter)]
            for k, done in enumerate(outputs(values, own_pairs)):
                own[group, k, member, at] = done

        tiles(body)

        @pl.when(is_inner)
        def _():
            copy_near(group).start()

    def third_stage(group):
        @pl.when(is_inner)
        def _():
            copy_raw(group).wait_recv()

            def body(member, at, first):
                values = [(raw[group, a, 0, member, at], raw[group, a, 1, member, at]) for a in range(quarter)]
                for k, done in enumerate(outputs(values, near_pairs)):
                    both[group, k, member, at] = done + own[group, k, member, at]

            tiles(body)
            copy_far_outer(group).start()
            copy_far(group).start()

    length = STEPS * LANES * GAP * devices
    lanes = lax.broadcasted_iota(jnp.int32, (tall, LANES), 1)
    lines = lax.broadcasted_iota(jnp.int32, (tall, LANES), 0)
    base = plane.astype(jnp.float32) * 0.25 - 0.5

    def finish(group, gather):
        def body(member, at, first):
            row = (place * SPLIT + group % SPLIT) * depth + first
            slot = ((lines + row) * LANES + lanes) * GAP
            within = (slot + group // SPLIT).astype(jnp.float32) / length
            for kk in range(quarter):
                centred = (base + kk / devices) + within
                weight = jnp.exp(RATE * centred * centred) * length**-0.5
                total[group, kk, member, at] = gather(kk, member, at) * weight

        tiles(body)

    def edges(end):
        row = 0 if end else depth - 1
        shift = 1 if end else -1

        @pl.loop(0, quarter)
        def _(kk):
            for p in range(RADIX):
                edge[kk, p : p + 1] = total[p * SPLIT + (0 if end else SPLIT - 1), kk, :, row]

        @pl.loop(0, quarter)
        def _(kk):
            target = plane * quarter + kk - shift
            inside = jnp.logical_and(target >= 0, target < devices)

            @pl.when(jnp.logical_and(inside, target != me))
            def _():
                copy_edge(kk, end).start()

    def edges_sent(end):
        shift = 1 if end else -1

        @pl.loop(0, quarter)
        def _(kk):
            target = plane * quarter + kk - shift
            inside = jnp.logical_and(target >= 0, target < devices)

            @pl.when(jnp.logical_and(inside, target != me))
            def _():
                copy_edge(kk, end).wait_send()

    def last_stage(group):
        copy_far(group).wait_recv()

        @pl.when(is_outer)
        def _():
            copy_near(group).wait_recv()
            finish(
                group,
                lambda kk, member, at: own[group, plane * quarter + kk, member, at]
                + (arrived[group, 1, kk, member, at] + arrived[group, 0, kk, member, at]),
            )

        @pl.when(is_inner)
        def _():
            finish(
                group,
                lambda kk, member, at: both[group, plane * quarter + kk, member, at] + arrived[group, 0, kk, member, at],
            )

        @pl.when(group == groups - 1)
        def _():
            for end in range(2):
                @pl.when(place == (0 if end else quarter - 1))
                def _():
                    edges(end)

        @pl.loop(1, quarter)
        def _(step):
            copy_b(group, beside(step)).start()

        out_ref[group, place] = total[group, place]

    stages = ((0, first_stage), (1, second_stage), (3, third_stage), (6, last_stage))

    @pl.loop(0, groups + 6)
    def _(turn):
        for lag, stage in stages:
            @pl.when(jnp.logical_and(turn >= lag, turn < groups + lag))
            def _():
                stage(turn - lag)

    for end in range(2):
        sender = 0 if end else quarter - 1
        bound = devices - 1 if end else 0

        @pl.when(me == bound)
        def _():
            halo_ref[end] = jnp.zeros(halo_ref.shape[1:], jnp.float32)

        @pl.when(jnp.logical_and(me != bound, place == sender))
        def _():
            halo_ref[end] = edge[sender + (1 if end else -1)]

        @pl.when(jnp.logical_and(me != bound, place != sender))
        def _():
            copy_edge(0, end).wait_recv()

    @pl.loop(0, groups)
    def _(group):
        whole(out_ref, group, sem_sb, sem_rb).wait_recv()

    for end in range(2):
        @pl.when(place == (0 if end else quarter - 1))
        def _():
            edges_sent(end)

    @pl.loop(0, groups)
    def _(group):
        whole(send_a, group, sem_sa, sem_ra).wait_send()
        whole(total, group, sem_sb, sem_rb).wait_send()

        @pl.when(is_outer)
        def _():
            copy_raw(group).wait_send()

        @pl.when(is_inner)
        def _():
            copy_far(group).wait_send()
            copy_far_outer(group).wait_send()
            copy_near(group).wait_send()


def across(samples, inner, outer):
    devices = inner * outer
    seg = samples.shape[2]
    length = seg * devices
    me = lax.axis_index("inner") * outer + lax.axis_index("outer")
    quarter = devices // 4
    depth = STEPS // (quarter * SPLIT)
    per = 1
    x = samples.reshape(2, RADIX, STEPS, LANES)

    def phase(number, order):
        angle = number.astype(jnp.float32) * (-TAU / order)
        return jnp.cos(angle), jnp.sin(angle)

    f = lax.broadcasted_iota(jnp.int32, (STEPS, LANES), 0)
    u = jnp.stack(phase(f * (lax.broadcasted_iota(jnp.int32, (STEPS, LANES), 1) * devices + me), length // RADIX))
    p = lax.broadcasted_iota(jnp.int32, (RADIX, LANES), 0)
    v = jnp.stack(phase(p * (lax.broadcasted_iota(jnp.int32, (RADIX, LANES), 1) * devices + me), length))
    g = lax.broadcasted_iota(jnp.int32, (LANES, LANES), 0)
    order = LANES * devices
    number = g * (lax.broadcasted_iota(jnp.int32, (LANES, LANES), 1) * devices + me) % order
    cosine, sine = phase(number, order)
    last = jnp.concatenate(
        [jnp.concatenate([cosine, -sine], axis=1), jnp.concatenate([sine, cosine], axis=1)], axis=0
    )
    vmem = pl.BlockSpec(memory_space=pltpu.VMEM)
    first = (GROUPS, quarter, 2, per, depth, LANES)
    block = (GROUPS, quarter, per, depth, LANES)
    wide = (GROUPS, devices, per, depth, LANES)
    return pl.pallas_call(
        functools.partial(across_kernel, inner, outer),
        out_shape=(
            jax.ShapeDtypeStruct(block, jnp.float32),
            jax.ShapeDtypeStruct((2, RADIX, LANES), jnp.float32),
        ),
        in_specs=[pl.BlockSpec(memory_space=pltpu.HBM)] * 2 + [vmem] * 3,
        out_specs=(vmem, vmem),
        scratch_shapes=[
            pltpu.VMEM(x.shape, jnp.float32),
            pltpu.VMEM((RADIX, 4, STEPS, STEPS), jnp.bfloat16),
            pltpu.VMEM((RADIX, STEPS, 2 * LANES), jnp.float32),
            pltpu.VMEM((2, STEPS, LANES), jnp.float32),
            pltpu.VMEM(first, jnp.float32),
            pltpu.VMEM(first, jnp.float32),
            pltpu.VMEM(first, jnp.float32),
            pltpu.VMEM(wide, jnp.float32),
            pltpu.VMEM(wide, jnp.float32),
            pltpu.VMEM((GROUPS, 2, quarter, per, depth, LANES), jnp.float32),
            pltpu.VMEM(block, jnp.float32),
            pltpu.VMEM((quarter, RADIX, LANES), jnp.float32),
        ]
        + [pltpu.SemaphoreType.DMA((2,)), pltpu.SemaphoreType.DMA((RADIX,))]
        + [pltpu.SemaphoreType.DMA((GROUPS,))] * 4
        + [pltpu.SemaphoreType.DMA((GROUPS, 3)), pltpu.SemaphoreType.DMA((GROUPS, 2))]
        + [pltpu.SemaphoreType.DMA((GROUPS,))] * 2
        + [pltpu.SemaphoreType.DMA((quarter,)), pltpu.SemaphoreType.DMA((2,))],
        compiler_params=pltpu.CompilerParams(
            collective_id=0, has_side_effects=True, vmem_limit_bytes=48 * 2**20
        ),
    )(x, jnp.asarray(stage_table()), u, v, last)


def gram_kernel(inner, outer, real_ref, halo_ref, index_ref, offset_ref, weight_ref, order_ref, z_ref, gram_ref, field, ordered, sem):
    devices = inner * outer
    groups, _, per, depth, _ = real_ref.shape

    @pl.loop(0, devices // 4)
    def _(e):
        for share in range(SPLIT):
            at = pl.ds(pl.multiple_of(8 + (e * SPLIT + share) * depth, math.gcd(8, depth)), depth)
            for p in range(GAP):
                field[p, at, :] = real_ref[p * SPLIT + share, e, 0]

    field[:, 7:8, :] = halo_ref[0][:, None, :]
    field[:, STEPS + 8 : STEPS + 9, :] = halo_ref[1][:, None, :]

    width = 2 * LANES
    share = width // GAP
    run = lax.broadcasted_iota(jnp.int32, (STEPS, LANES), 1) // share
    for column in range(LANES // share):
        packed = []
        for first in range(0, GAP, LANES // share):
            piece = None
            for place in range(LANES // share):
                value = field[first + place, 8 : STEPS + 8, :]
                turn = (place - column) * share % LANES
                value = pltpu.roll(value, turn, 1) if turn else value
                piece = value if piece is None else jnp.where(run == place, value, piece)
            packed.append(piece)
        rest = jnp.concatenate(packed, axis=1)
        block = None
        for _ in range(2):
            piece = rest.astype(jnp.bfloat16)
            rest = rest - piece.astype(jnp.float32)
            product = jnp.dot(piece, order_ref[...], preferred_element_type=jnp.float32)
            block = product if block is None else block + product
        for side in range(2):
            ordered[pl.ds(2 * column + side, STEPS, stride=GAP), :] = block[:, side * LANES : (side + 1) * LANES]

    leave = pltpu.make_async_copy(ordered, z_ref, sem)
    leave.start()

    lane = lax.broadcasted_iota(jnp.int32, (8, LANES), 1)

    @pl.loop(0, STEPS // 8, unroll=2)
    def _(tile):
        row = pl.multiple_of(tile * 8, 8)
        index = index_ref[pl.ds(row, 8)]
        offset = offset_ref[pl.ds(row, 8)]
        samples = {}
        for p in range(GAP):
            now = field[p, pl.ds(row + 8, 8)]
            before = field[p, pl.ds(row + 7, 8)]
            after = field[p, pl.ds(row + 9, 8)]
            for slot in (-2, -1, 0, 1, 2):
                place = GAP * slot + p
                if place < 1 - HALF or place > HALF + GAP - 1:
                    continue
                if slot < 0:
                    value = pltpu.roll(jnp.where(lane >= LANES + slot, before, now), -slot, 1)
                elif slot > 0:
                    value = pltpu.roll(jnp.where(lane < slot, after, now), LANES - slot, 1)
                else:
                    value = now
                samples[place] = value
        window = [samples[place] for place in range(1 - HALF, HALF + GAP)]
        for bit in (4, 2, 1):
            chosen = (index & bit) != 0
            window = [jnp.where(chosen, b, a) for a, b in zip(window[:-bit], window[bit:])]
        total = jnp.zeros((8, LANES), jnp.float32)
        for tap in range(2 * HALF):
            total += window[tap] * jnp.take_along_axis(weight_ref[tap], offset, axis=1)
        gram_ref[pl.ds(row, 8)] = total

    leave.wait()


def local(inner, outer, samples, gram_index, gram_offset):
    real, halo = across(samples, inner, outer)
    rows = (STEPS, LANES)
    z, gram = pl.pallas_call(
        functools.partial(gram_kernel, inner, outer),
        out_shape=(
            jax.ShapeDtypeStruct((STEPS * GAP, LANES), jnp.float32),
            jax.ShapeDtypeStruct(rows, jnp.float32),
        ),
        in_specs=[pl.BlockSpec(memory_space=pltpu.VMEM)] * 6,
        out_specs=(pl.BlockSpec(memory_space=pltpu.HBM), pl.BlockSpec(memory_space=pltpu.VMEM)),
        scratch_shapes=[
            pltpu.VMEM((GAP, STEPS + 16, LANES), jnp.float32),
            pltpu.VMEM((STEPS * GAP, LANES), jnp.float32),
            pltpu.SemaphoreType.DMA,
        ],
        compiler_params=pltpu.CompilerParams(vmem_limit_bytes=48 * 2**20),
    )(
        real, halo, gram_index.reshape(rows), gram_offset.reshape(rows),
        jnp.asarray(weight_table()), jnp.asarray(order_table()),
    )
    return z.reshape(-1), gram.reshape(-1)


def solution(mesh):
    return jax.shard_map(
        functools.partial(local, mesh.shape["inner"], mesh.shape["outer"]),
        mesh=mesh,
        in_specs=(P(None, ("inner", "outer"), None), P(("inner", "outer")), P(("inner", "outer"))),
        out_specs=(P(("inner", "outer")), P(("inner", "outer"))),
        check_vma=False,
    )
```

```python
import functools
import math

import jax
import jax.numpy as jnp
import numpy as np
from jax import lax
from jax.experimental import pallas as pl
from jax.experimental.pallas import tpu as pltpu
from jax.sharding import PartitionSpec as P

GAP = 8
HALF = 16
UPS = 32
LANES = 128
RADIX = 8
STEPS = 256
SPLIT = 2
GROUPS = RADIX * SPLIT
TAU = 2.0 * math.pi
RATE = 4.0
MESH = pl.DeviceIdType.MESH
NT = (((1,), (1,)), ((), ()))


def halves(x):
    high = x.astype(jnp.bfloat16)
    low = (x - high.astype(jnp.float32)).astype(jnp.bfloat16)
    return high, low


def np_halves(x):
    x = x.astype(np.float32)
    high = x.astype(jnp.bfloat16)
    low = (x - high.astype(np.float32)).astype(jnp.bfloat16)
    return high, low


def stage_table():
    p = np.arange(RADIX)[:, None, None]
    f = np.arange(STEPS)[None, :, None]
    t = np.arange(STEPS)[None, None, :]
    order = RADIX * STEPS
    angle = (t * (RADIX * f + p) % order) * (-TAU / order)
    return np.stack([*np_halves(np.cos(angle)), *np_halves(np.sin(angle))], axis=1)


def order_table():
    size = 2 * LANES
    p, l = np.divmod(np.arange(size), size // GAP)
    table = np.zeros((size, size), np.float32)
    table[np.arange(size), GAP * l + p] = 1.0
    return table.astype(jnp.bfloat16)


def weight_table():
    tap = np.arange(1 - HALF, HALF + 1)[:, None]
    distance = np.arange(LANES)[None, :] % UPS / UPS - tap
    spread = HALF / 2.0
    table = np.sinc(distance) * np.exp(-distance * distance / (2.0 * spread * spread))
    return np.broadcast_to(table.astype(np.float32)[:, None, :], (2 * HALF, 8, LANES)).copy()


def radix_8(parts):
    def add(u, v):
        return u[0] + v[0], u[1] + v[1]

    def sub(u, v):
        return u[0] - v[0], u[1] - v[1]

    def turn(u):
        return u[1], -u[0]

    def four(a, b, c, d):
        s, t, u, v = add(a, c), sub(a, c), add(b, d), turn(sub(b, d))
        return add(s, u), add(t, v), sub(s, u), sub(t, v)

    even = four(parts[0], parts[2], parts[4], parts[6])
    odd = four(parts[1], parts[3], parts[5], parts[7])
    r = math.sqrt(0.5)
    odd = (
        odd[0],
        ((odd[1][0] + odd[1][1]) * r, (odd[1][1] - odd[1][0]) * r),
        turn(odd[2]),
        ((odd[3][1] - odd[3][0]) * r, -(odd[3][0] + odd[3][1]) * r),
    )
    return [add(e, o) for e, o in zip(even, odd)] + [sub(e, o) for e, o in zip(even, odd)]


def transform(values):
    size = len(values)
    if size == 1:
        return values
    even, odd = transform(values[0::2]), transform(values[1::2])
    first, second = [], []
    for k in range(size // 2):
        (er, ei), (br, bi) = even[k], odd[k]
        if k == 0:
            tr, ti = br, bi
        elif 4 * k == size:
            tr, ti = bi, -br
        else:
            c, s = math.cos(TAU * k / size), -math.sin(TAU * k / size)
            tr, ti = br * c - bi * s, br * s + bi * c
        first.append((er + tr, ei + ti))
        second.append((er - tr, ei - ti))
    return first + second


def real_transform(values):
    size = len(values)
    even, odd = transform(values[0::2]), transform(values[1::2])
    first, second = [], []
    for k in range(size // 2):
        c, s = math.cos(TAU * k / size), -math.sin(TAU * k / size)
        t = odd[k][0] if k == 0 else odd[k][1] if 4 * k == size else odd[k][0] * c - odd[k][1] * s
        first.append(even[k][0] + t)
        second.append(even[k][0] - t)
    return first + second


def across_kernel(
    inner, outer, x_hbm, stage_hbm, u_ref, v_ref, last_ref, out_ref, halo_ref,
    x_ref, stage_ref, parts, rows, send_a, recv_a, raw, own, both, arrived, total, edge,
    sem_x, sem_t, sem_sa, sem_ra, sem_sw, sem_rw, sem_sp, sem_rp, sem_sb, sem_rb, sem_se, sem_re,
):
    devices = inner * outer
    me = lax.axis_index("inner") * outer + lax.axis_index("outer")
    groups, quarter, _, per, depth, _ = send_a.shape
    plane = me // quarter
    place = me % quarter
    near_plane = plane + 1 - 2 * (plane % 2)
    far_plane = 3 - plane
    far_outer = far_plane + 1 - 2 * (far_plane % 2)
    is_outer = jnp.logical_or(plane == 0, plane == 3)
    is_inner = jnp.logical_not(is_outer)

    def where(device):
        return (device // outer, device % outer)

    def beside(step):
        return plane * quarter + (place + step) % quarter

    def load_x(part):
        return pltpu.make_async_copy(x_hbm.at[part], x_ref.at[part], sem_x.at[part])

    def load_table(p):
        return pltpu.make_async_copy(stage_hbm.at[p], stage_ref.at[p], sem_t.at[p])

    for part in range(2):
        load_x(part).start()

    @pl.loop(0, RADIX)
    def _(p):
        load_table(p).start()

    barrier = pltpu.get_barrier_semaphore()

    @pl.loop(1, devices)
    def _(step):
        pl.semaphore_signal(barrier, inc=1, device_id=where((me + step) % devices), device_id_type=MESH)

    for part in range(2):
        load_x(part).wait()

    @pl.loop(0, STEPS // 32)
    def _(tile):
        at = pl.ds(pl.multiple_of(tile * 32, 32), 32)
        done = radix_8([(x_ref[0, q, at], x_ref[1, q, at]) for q in range(RADIX)])
        for p in range(RADIX):
            parts[p, at, :LANES] = done[p][0]
            parts[p, at, LANES:] = done[p][1]

    def dot(a, b):
        return jnp.dot(a, b, preferred_element_type=jnp.float32)

    def dot_nt(a, b):
        return lax.dot_general(a, b, NT, preferred_element_type=jnp.float32)

    def send(source, target_ref, sent, here, device):
        return pltpu.make_async_remote_copy(
            src_ref=source, dst_ref=target_ref, send_sem=sent, recv_sem=here,
            device_id=where(device), device_id_type=MESH,
        )

    def copy_a(group, target):
        return send(
            send_a.at[group, target % quarter], recv_a.at[group, place], sem_sa.at[group], sem_ra.at[group], target
        )

    def copy_b(group, target):
        return send(
            total.at[group, target % quarter], out_ref.at[group, place], sem_sb.at[group], sem_rb.at[group], target
        )

    def copy_raw(group):
        return send(
            recv_a.at[group], raw.at[group], sem_sw.at[group], sem_rw.at[group], near_plane * quarter + place
        )

    def copy_part(source, group, slot, number, to_plane):
        return send(
            source.at[group, pl.ds(to_plane * quarter, quarter)], arrived.at[group, slot],
            sem_sp.at[group, number], sem_rp.at[group, slot], to_plane * quarter + place,
        )

    def copy_far(group):
        return copy_part(both, group, 0, 0, far_plane)

    def copy_far_outer(group):
        return copy_part(both, group, 0, 1, far_outer)

    def copy_near(group):
        return copy_part(own, group, 1, 2, near_plane)

    def whole(ref, group, sem_sent, sem_here):
        part = ref.at[group, pl.ds(0, quarter - 1)]
        return send(part, part, sem_sent.at[group], sem_here.at[group], beside(1))

    def copy_edge(kk, end):
        target = (plane * quarter + kk - (1 if end else -1) + devices) % devices
        return send(edge.at[kk], halo_ref.at[end], sem_se.at[kk], sem_re.at[end], target)

    last_high, last_low = halves(last_ref[...])

    def spectrum(p):
        load_table(p).wait()
        high, low = halves(parts[p])
        cos_high, cos_low, sin_high, sin_low = (stage_ref[p, i] for i in range(4))
        by_cos = dot(cos_high, high) + dot(cos_high, low) + dot(cos_low, high)
        by_sin = dot(sin_high, high) + dot(sin_high, low) + dot(sin_low, high)
        real = by_cos[:, :LANES] - by_sin[:, LANES:]
        imag = by_cos[:, LANES:] + by_sin[:, :LANES]
        vr, vi = v_ref[0, pl.ds(p, 1)], v_ref[1, pl.ds(p, 1)]
        ur, ui = u_ref[0], u_ref[1]
        tr, ti = ur * vr - ui * vi, ur * vi + ui * vr
        both = jnp.concatenate([real * tr - imag * ti, real * ti + imag * tr], axis=1)
        high, low = halves(both)
        z = dot_nt(last_high, high) + dot_nt(last_high, low) + dot_nt(last_low, high)
        for part in range(2):
            block = z[part * LANES : (part + 1) * LANES]
            for lane_half in range(2):
                rows[part, pl.ds(lane_half, LANES, stride=2), :] = block[:, lane_half * LANES : (lane_half + 1) * LANES]
            value = rows[part].reshape(quarter, SPLIT, depth, LANES)
            for share in range(SPLIT):
                send_a[p * SPLIT + share, :, part, 0] = value[:, share]

    def spectra(group):
        @pl.when(group % SPLIT == 0)
        def _():
            spectrum(group // SPLIT)

        recv_a[group, place] = send_a[group, place]

    def factors(which):
        pairs = []
        for v in range(4):
            turns = (which * v) % 4
            real = jnp.where(turns == 0, 1.0, jnp.where(turns == 2, -1.0, 0.0))
            imag = jnp.where(turns == 1, -1.0, jnp.where(turns == 3, 1.0, 0.0))
            pairs.append((real, imag))
        return pairs

    def outputs(values, pairs):
        result = [None] * devices
        for v in range(4):
            turned = []
            for a, (vr, vi) in enumerate(values):
                c, s = math.cos(TAU * a * v / devices), -math.sin(TAU * a * v / devices)
                turned.append((vr, vi) if a * v == 0 else (vr * c - vi * s, vr * s + vi * c))
            for u, (real, imag) in enumerate(transform(turned)):
                result[4 * u + v] = real if v == 0 else real * pairs[v][0] - imag * pairs[v][1]
        return result

    tall = min(8, depth)

    def tiles(body):
        @pl.loop(0, per)
        def _(member):
            @pl.loop(0, depth // tall)
            def _(tile):
                body(member, pl.ds(pl.multiple_of(tile * tall, tall), tall), tile * tall)

    own_pairs, near_pairs = factors(plane), factors(near_plane)

    def first_stage(group):
        spectra(group)

        @pl.when(group == 0)
        def _():
            pl.semaphore_wait(barrier, devices - 1)

        @pl.loop(1, quarter)
        def _(step):
            copy_a(group, beside(step)).start()

    def second_stage(group):
        whole(recv_a, group, sem_sa, sem_ra).wait_recv()

        @pl.when(is_outer)
        def _():
            copy_raw(group).start()

        def body(member, at, first):
            values = [(recv_a[group, a, 0, member, at], recv_a[group, a, 1, member, at]) for a in range(quarter)]
            for k, done in enumerate(outputs(values, own_pairs)):
                own[group, k, member, at] = done

        tiles(body)

        @pl.when(is_inner)
        def _():
            copy_near(group).start()

    def third_stage(group):
        @pl.when(is_inner)
        def _():
            copy_raw(group).wait_recv()

            def body(member, at, first):
                values = [(raw[group, a, 0, member, at], raw[group, a, 1, member, at]) for a in range(quarter)]
                for k, done in enumerate(outputs(values, near_pairs)):
                    both[group, k, member, at] = done + own[group, k, member, at]

            tiles(body)
            copy_far_outer(group).start()
            copy_far(group).start()

    length = STEPS * LANES * GAP * devices
    lanes = lax.broadcasted_iota(jnp.int32, (tall, LANES), 1)
    lines = lax.broadcasted_iota(jnp.int32, (tall, LANES), 0)
    base = plane.astype(jnp.float32) * 0.25 - 0.5

    def finish(group, gather):
        def body(member, at, first):
            row = (place * SPLIT + group % SPLIT) * depth + first
            slot = ((lines + row) * LANES + lanes) * GAP
            within = (slot + group // SPLIT).astype(jnp.float32) / length
            for kk in range(quarter):
                centred = (base + kk / devices) + within
                weight = jnp.exp(RATE * centred * centred) * length**-0.5
                total[group, kk, member, at] = gather(kk, member, at) * weight

        tiles(body)

    def edges(end):
        row = 0 if end else depth - 1
        shift = 1 if end else -1

        @pl.loop(0, quarter)
        def _(kk):
            for p in range(RADIX):
                edge[kk, p : p + 1] = total[p * SPLIT + (0 if end else SPLIT - 1), kk, :, row]

        @pl.loop(0, quarter)
        def _(kk):
            target = plane * quarter + kk - shift
            inside = jnp.logical_and(target >= 0, target < devices)

            @pl.when(jnp.logical_and(inside, target != me))
            def _():
                copy_edge(kk, end).start()

    def edges_sent(end):
        shift = 1 if end else -1

        @pl.loop(0, quarter)
        def _(kk):
            target = plane * quarter + kk - shift
            inside = jnp.logical_and(target >= 0, target < devices)

            @pl.when(jnp.logical_and(inside, target != me))
            def _():
                copy_edge(kk, end).wait_send()

    def last_stage(group):
        copy_far(group).wait_recv()

        @pl.when(is_outer)
        def _():
            copy_near(group).wait_recv()
            finish(
                group,
                lambda kk, member, at: own[group, plane * quarter + kk, member, at]
                + (arrived[group, 1, kk, member, at] + arrived[group, 0, kk, member, at]),
            )

        @pl.when(is_inner)
        def _():
            finish(
                group,
                lambda kk, member, at: both[group, plane * quarter + kk, member, at] + arrived[group, 0, kk, member, at],
            )

        @pl.when(group == groups - 1)
        def _():
            for end in range(2):
                @pl.when(place == (0 if end else quarter - 1))
                def _():
                    edges(end)

        @pl.loop(1, quarter)
        def _(step):
            copy_b(group, beside(step)).start()

        out_ref[group, place] = total[group, place]

    stages = ((0, first_stage), (1, second_stage), (3, third_stage), (6, last_stage))

    @pl.loop(0, groups + 6)
    def _(turn):
        for lag, stage in stages:
            @pl.when(jnp.logical_and(turn >= lag, turn < groups + lag))
            def _():
                stage(turn - lag)

    for end in range(2):
        sender = 0 if end else quarter - 1
        bound = devices - 1 if end else 0

        @pl.when(me == bound)
        def _():
            halo_ref[end] = jnp.zeros(halo_ref.shape[1:], jnp.float32)

        @pl.when(jnp.logical_and(me != bound, place == sender))
        def _():
            halo_ref[end] = edge[sender + (1 if end else -1)]

        @pl.when(jnp.logical_and(me != bound, place != sender))
        def _():
            copy_edge(0, end).wait_recv()

    @pl.loop(0, groups)
    def _(group):
        whole(out_ref, group, sem_sb, sem_rb).wait_recv()

    for end in range(2):
        @pl.when(place == (0 if end else quarter - 1))
        def _():
            edges_sent(end)

    @pl.loop(0, groups)
    def _(group):
        whole(send_a, group, sem_sa, sem_ra).wait_send()
        whole(total, group, sem_sb, sem_rb).wait_send()

        @pl.when(is_outer)
        def _():
            copy_raw(group).wait_send()

        @pl.when(is_inner)
        def _():
            copy_far(group).wait_send()
            copy_far_outer(group).wait_send()
            copy_near(group).wait_send()


def across(samples, inner, outer):
    devices = inner * outer
    seg = samples.shape[2]
    length = seg * devices
    me = lax.axis_index("inner") * outer + lax.axis_index("outer")
    quarter = devices // 4
    depth = STEPS // (quarter * SPLIT)
    per = 1
    x = samples.reshape(2, RADIX, STEPS, LANES)

    def phase(number, order):
        angle = number.astype(jnp.float32) * (-TAU / order)
        return jnp.cos(angle), jnp.sin(angle)

    f = lax.broadcasted_iota(jnp.int32, (STEPS, LANES), 0)
    u = jnp.stack(phase(f * (lax.broadcasted_iota(jnp.int32, (STEPS, LANES), 1) * devices + me), length // RADIX))
    p = lax.broadcasted_iota(jnp.int32, (RADIX, LANES), 0)
    v = jnp.stack(phase(p * (lax.broadcasted_iota(jnp.int32, (RADIX, LANES), 1) * devices + me), length))
    g = lax.broadcasted_iota(jnp.int32, (LANES, LANES), 0)
    order = LANES * devices
    number = g * (lax.broadcasted_iota(jnp.int32, (LANES, LANES), 1) * devices + me) % order
    cosine, sine = phase(number, order)
    last = jnp.concatenate(
        [jnp.concatenate([cosine, -sine], axis=1), jnp.concatenate([sine, cosine], axis=1)], axis=0
    )
    vmem = pl.BlockSpec(memory_space=pltpu.VMEM)
    first = (GROUPS, quarter, 2, per, depth, LANES)
    block = (GROUPS, quarter, per, depth, LANES)
    wide = (GROUPS, devices, per, depth, LANES)
    return pl.pallas_call(
        functools.partial(across_kernel, inner, outer),
        out_shape=(
            jax.ShapeDtypeStruct(block, jnp.float32),
            jax.ShapeDtypeStruct((2, RADIX, LANES), jnp.float32),
        ),
        in_specs=[pl.BlockSpec(memory_space=pltpu.HBM)] * 2 + [vmem] * 3,
        out_specs=(vmem, vmem),
        scratch_shapes=[
            pltpu.VMEM(x.shape, jnp.float32),
            pltpu.VMEM((RADIX, 4, STEPS, STEPS), jnp.bfloat16),
            pltpu.VMEM((RADIX, STEPS, 2 * LANES), jnp.float32),
            pltpu.VMEM((2, STEPS, LANES), jnp.float32),
            pltpu.VMEM(first, jnp.float32),
            pltpu.VMEM(first, jnp.float32),
            pltpu.VMEM(first, jnp.float32),
            pltpu.VMEM(wide, jnp.float32),
            pltpu.VMEM(wide, jnp.float32),
            pltpu.VMEM((GROUPS, 2, quarter, per, depth, LANES), jnp.float32),
            pltpu.VMEM(block, jnp.float32),
            pltpu.VMEM((quarter, RADIX, LANES), jnp.float32),
        ]
        + [pltpu.SemaphoreType.DMA((2,)), pltpu.SemaphoreType.DMA((RADIX,))]
        + [pltpu.SemaphoreType.DMA((GROUPS,))] * 4
        + [pltpu.SemaphoreType.DMA((GROUPS, 3)), pltpu.SemaphoreType.DMA((GROUPS, 2))]
        + [pltpu.SemaphoreType.DMA((GROUPS,))] * 2
        + [pltpu.SemaphoreType.DMA((quarter,)), pltpu.SemaphoreType.DMA((2,))],
        compiler_params=pltpu.CompilerParams(
            collective_id=0, has_side_effects=True, vmem_limit_bytes=62 * 2**20
        ),
    )(x, jnp.asarray(stage_table()), u, v, last)


def gram_kernel(inner, outer, real_ref, halo_ref, index_ref, offset_ref, weight_ref, order_ref, z_ref, gram_ref, field, ordered, sem):
    devices = inner * outer
    groups, _, per, depth, _ = real_ref.shape

    @pl.loop(0, devices // 4)
    def _(e):
        for share in range(SPLIT):
            at = pl.ds(pl.multiple_of(8 + (e * SPLIT + share) * depth, math.gcd(8, depth)), depth)
            for p in range(GAP):
                field[p, at, :] = real_ref[p * SPLIT + share, e, 0]

    field[:, 7:8, :] = halo_ref[0][:, None, :]
    field[:, STEPS + 8 : STEPS + 9, :] = halo_ref[1][:, None, :]

    width = 2 * LANES
    share = width // GAP
    run = lax.broadcasted_iota(jnp.int32, (STEPS, LANES), 1) // share
    for column in range(LANES // share):
        packed = []
        for first in range(0, GAP, LANES // share):
            piece = None
            for place in range(LANES // share):
                value = field[first + place, 8 : STEPS + 8, :]
                turn = (place - column) * share % LANES
                value = pltpu.roll(value, turn, 1) if turn else value
                piece = value if piece is None else jnp.where(run == place, value, piece)
            packed.append(piece)
        rest = jnp.concatenate(packed, axis=1)
        block = None
        for _ in range(2):
            piece = rest.astype(jnp.bfloat16)
            rest = rest - piece.astype(jnp.float32)
            product = jnp.dot(piece, order_ref[...], preferred_element_type=jnp.float32)
            block = product if block is None else block + product
        for side in range(2):
            ordered[pl.ds(2 * column + side, STEPS, stride=GAP), :] = block[:, side * LANES : (side + 1) * LANES]

    leave = pltpu.make_async_copy(ordered, z_ref, sem)
    leave.start()

    lane = lax.broadcasted_iota(jnp.int32, (8, LANES), 1)

    @pl.loop(0, STEPS // 8, unroll=2)
    def _(tile):
        row = pl.multiple_of(tile * 8, 8)
        index = index_ref[pl.ds(row, 8)]
        offset = offset_ref[pl.ds(row, 8)]
        samples = {}
        for p in range(GAP):
            now = field[p, pl.ds(row + 8, 8)]
            before = field[p, pl.ds(row + 7, 8)]
            after = field[p, pl.ds(row + 9, 8)]
            for slot in (-2, -1, 0, 1, 2):
                place = GAP * slot + p
                if place < 1 - HALF or place > HALF + GAP - 1:
                    continue
                if slot < 0:
                    value = pltpu.roll(jnp.where(lane >= LANES + slot, before, now), -slot, 1)
                elif slot > 0:
                    value = pltpu.roll(jnp.where(lane < slot, after, now), LANES - slot, 1)
                else:
                    value = now
                samples[place] = value
        window = [samples[place] for place in range(1 - HALF, HALF + GAP)]
        for bit in (4, 2, 1):
            chosen = (index & bit) != 0
            window = [jnp.where(chosen, b, a) for a, b in zip(window[:-bit], window[bit:])]
        total = jnp.zeros((8, LANES), jnp.float32)
        for tap in range(2 * HALF):
            total += window[tap] * jnp.take_along_axis(weight_ref[tap], offset, axis=1)
        gram_ref[pl.ds(row, 8)] = total

    leave.wait()


def local(inner, outer, samples, gram_index, gram_offset):
    real, halo = across(samples, inner, outer)
    rows = (STEPS, LANES)
    z, gram = pl.pallas_call(
        functools.partial(gram_kernel, inner, outer),
        out_shape=(
            jax.ShapeDtypeStruct((STEPS * GAP, LANES), jnp.float32),
            jax.ShapeDtypeStruct(rows, jnp.float32),
        ),
        in_specs=[pl.BlockSpec(memory_space=pltpu.VMEM)] * 6,
        out_specs=(pl.BlockSpec(memory_space=pltpu.HBM), pl.BlockSpec(memory_space=pltpu.VMEM)),
        scratch_shapes=[
            pltpu.VMEM((GAP, STEPS + 16, LANES), jnp.float32),
            pltpu.VMEM((STEPS * GAP, LANES), jnp.float32),
            pltpu.SemaphoreType.DMA,
        ],
        compiler_params=pltpu.CompilerParams(vmem_limit_bytes=48 * 2**20),
    )(
        real, halo, gram_index.reshape(rows), gram_offset.reshape(rows),
        jnp.asarray(weight_table()), jnp.asarray(order_table()),
    )
    return z.reshape(-1), gram.reshape(-1)


def solution(mesh):
    return jax.shard_map(
        functools.partial(local, mesh.shape["inner"], mesh.shape["outer"]),
        mesh=mesh,
        in_specs=(P(None, ("inner", "outer"), None), P(("inner", "outer")), P(("inner", "outer"))),
        out_specs=(P(("inner", "outer")), P(("inner", "outer"))),
        check_vma=False,
    )
```
